512 devices in a mesh: ctx: 16 (over x, z_hi, core), ch: 32 (over z_lo, y).
Axes of the slice: x: 4, y: 8, z: 8 (z_hi: 2, z_lo: 4; z = z_hi * 4 + z_lo), core: 2. Of those that a mesh axis runs over, the one named last changes fastest.
Arguments:
- tokens: bfloat16 [16384, 4096], P('ctx', 'ch'), may hold values from -6 to 6
- in_weights: bfloat16 [3, 4096, 4096], P(None, None, 'ch'), may hold values from -0.09375 to 0.09375
- short_taps: float32 [3, 7, 4096], P(None, None, 'ch'), may hold values from -2 to 2
- residues: float32 [4096, 16], P('ch'), may hold values from -4 to 4
- decays: float32 [4096, 16], P('ch'), may hold values from 3.0517578e-05 to 0.03125
- skip_gain: float32 [4096], P('ch'), may hold values from 0.5 to 1.5
Outputs:
- mixed: float32 [16384, 4096], P('ctx', 'ch')
The draws below stay inside these ranges and needn't reach their ends.
All inputs are finite; a program needn't handle non-finite values.
Results may differ from the reference program's by a relative error of at most 0.0003.
Values may be sent and summed in bfloat16 or wider, within the bound.
No kernel may reach another device: no remote copies, remote signals or barrier semaphores. Data moves between devices by JAX's collectives and lax.ppermute only.
A program may use at most 64 MiB of HBM per device.

```python
import math
import jax
import jax.numpy as jnp

D = 4096
CHANNELS = 4096
MODES = 16
TAPS = 7
SEQ = 16384


def level_of(own_key, shape, split, low, top_value):
    def one(axis_at, blocks):
        steps = jax.random.uniform(jax.random.fold_in(jax.random.fold_in(own_key, 6), axis_at), (blocks,), jnp.float32, low / len(split), top_value / len(split))
        return jnp.repeat(jnp.exp(steps), shape[axis_at] // blocks).reshape((-1,) + (1,) * (len(shape) - axis_at - 1))

    factor_of = one(*split[0])
    for cut in split[1:]:
        factor_of = factor_of * one(*cut)
    return factor_of


def centred(stream_key, dims, spread, most, cuts=(), kind=jnp.bfloat16):
    level = level_of(stream_key, dims, cuts, -0.22, 0.18) if cuts else 1.0
    result = jax.random.normal(stream_key, dims, jnp.float32) * spread * level
    return jnp.minimum(jnp.maximum(result, -most), most).astype(kind)


def setup_inputs(seed: int = 0) -> dict:
    splits = jax.random.split(jax.random.key(seed), 7)
    tokens = centred(splits[0], (SEQ, D), 1.0, 6.0, ((0, 16), (1, 32)))
    in_weights = centred(splits[1], (3, D, CHANNELS), D ** -0.5, 0.09375, ((2, 32),))
    short_taps = centred(splits[2], (3, TAPS, CHANNELS), TAPS ** -0.5, 2.0, ((2, 32),), jnp.float32)
    residues = centred(splits[3], (CHANNELS, MODES), 1.0, 4.0, ((0, 32),), jnp.float32)
    decays = jnp.clip(jnp.exp(math.log(0.03125) - 6.931472 * jax.random.uniform(splits[4], (CHANNELS, MODES), jnp.float32) ** level_of(splits[4], (CHANNELS, MODES), ((0, 32),), -0.2, 0.2)), 3.0517578125e-05, 0.03125)
    skip_gain = jnp.clip(0.5 + 1.0 * jax.random.uniform(splits[5], (CHANNELS,), jnp.float32) ** level_of(splits[5], (CHANNELS,), ((0, 32),), -0.2, 0.2), 0.5, 1.5)
    return dict(tokens=tokens, in_weights=in_weights, short_taps=short_taps, residues=residues, decays=decays, skip_gain=skip_gain)


def reference(tokens, in_weights, short_taps, residues, decays, skip_gain):
    projected = jnp.stack([jnp.dot(tokens, in_weights[stream], preferred_element_type=jnp.float32) for stream in range(3)])
    seq_len = projected.shape[1]
    padded = jnp.pad(projected, ((0, 0), (TAPS - 1, 0), (0, 0)))
    filtered = jnp.zeros_like(projected)
    for offset in range(TAPS):
        filtered = filtered + short_taps[:, offset][:, None, :] * padded[:, offset:offset + seq_len, :]
    gated = filtered[1] * filtered[2]
    positions = jnp.arange(seq_len, dtype=jnp.int32).astype(jnp.float32)[:, None]
    weights = residues * jnp.sqrt(2.0 * decays / MODES)
    long_filter = jnp.zeros_like(gated)
    for which_mode in range(MODES):
        long_filter = long_filter + weights[:, which_mode][None, :] * jnp.exp(-decays[:, which_mode][None, :] * positions)
    spectrum = jnp.fft.rfft(gated, n=2 * seq_len, axis=0) * jnp.fft.rfft(long_filter, n=2 * seq_len, axis=0)
    convolved = jnp.fft.irfft(spectrum, n=2 * seq_len, axis=0)[:seq_len]
    return filtered[0] * (convolved + skip_gain[None, :] * gated)
```

```python
import functools

import jax
import jax.numpy as jnp
from jax import lax
from jax.experimental import pallas as pl
from jax.experimental.pallas import tpu as pltpu
from jax.sharding import PartitionSpec as P

MODES = 16
TAPS = 7
HALO = 8
CHUNKS = 8
UNROLL = 8
LANES = 128


def wide(row):
    return jnp.broadcast_to(row, (CHUNKS, LANES))


def local_kernel(length, proj, taps, weights, decays, skip, first, direct, starts, last, ends):
    poles = [wide(jnp.exp(-decays[m : m + 1, :])) for m in range(MODES)]
    gains = [wide(weights[m : m + 1, :]) for m in range(MODES)]
    skip_row = wide(skip[0:1, :])

    def steps(at, states):
        states = list(states)
        at = at * UNROLL
        rows = [
            [
                proj[s, pl.ds(at + HALO - (TAPS - 1) + k, CHUNKS, stride=length), :]
                for k in range(UNROLL + TAPS - 1)
            ]
            for s in range(3)
        ]
        coef = [[wide(taps[s, j : j + 1, :]) for j in range(TAPS)] for s in range(3)]
        for u in range(UNROLL):
            filtered = [sum(coef[s][j] * rows[s][u + j] for j in range(TAPS)) for s in range(3)]
            gated = filtered[1] * filtered[2]
            total = skip_row * gated
            for m in range(MODES):
                states[m] = poles[m] * states[m] + gated
                total = total + gains[m] * states[m]
            here = pl.ds(pl.multiple_of((at + u) * CHUNKS, CHUNKS), CHUNKS)
            first[here, :] = filtered[0]
            direct[here, :] = filtered[0] * total
        return tuple(states)

    zero = jnp.zeros((CHUNKS, LANES), jnp.float32)
    states = lax.fori_loop(0, length // UNROLL, steps, (zero,) * MODES)
    for m in range(MODES):
        ends[m * CHUNKS : (m + 1) * CHUNKS, :] = states[m]
    over = jnp.exp(-decays[...] * float(length))
    carry = jnp.zeros((MODES, LANES), jnp.float32)
    for c in range(CHUNKS):
        starts[c] = carry
        carry = over * carry + ends[pl.ds(c, MODES, stride=CHUNKS), :]
    last[...] = carry


def local_part(proj, taps, weights, decays, skip):
    rows = proj.shape[1] - HALO
    width = proj.shape[2]
    flat = jax.ShapeDtypeStruct((rows, width), jnp.float32)
    column = lambda n: pl.BlockSpec((n, LANES), lambda i: (0, i))
    return pl.pallas_call(
        functools.partial(local_kernel, rows // CHUNKS),
        grid=(width // LANES,),
        in_specs=[
            pl.BlockSpec((3, rows + HALO, LANES), lambda i: (0, 0, i)),
            pl.BlockSpec((3, TAPS, LANES), lambda i: (0, 0, i)),
            column(MODES),
            column(MODES),
            column(1),
        ],
        out_specs=[
            column(rows),
            column(rows),
            pl.BlockSpec((CHUNKS, MODES, LANES), lambda i: (0, 0, i)),
            column(MODES),
        ],
        out_shape=[
            flat,
            flat,
            jax.ShapeDtypeStruct((CHUNKS, MODES, width), jnp.float32),
            jax.ShapeDtypeStruct((MODES, width), jnp.float32),
        ],
        scratch_shapes=[pltpu.VMEM((MODES * CHUNKS, LANES), jnp.float32)],
        compiler_params=pltpu.CompilerParams(vmem_limit_bytes=32 * 2**20),
        cost_estimate=pl.CostEstimate(
            flops=rows * width * 110, bytes_accessed=rows * width * 20, transcendentals=0
        ),
    )(proj, taps, weights, decays, skip)


def final_kernel(length, carried, first, direct, starts, weights, decays, out, begins):
    over = jnp.exp(-decays[...] * float(length))
    reach = jnp.ones_like(over)
    for c in range(CHUNKS):
        begins[pl.ds(c, MODES, stride=CHUNKS), :] = weights[...] * (starts[c] + reach * carried[...])
        reach = reach * over
    poles = [wide(jnp.exp(-decays[m : m + 1, :])) for m in range(MODES)]

    def steps(at, terms):
        terms = list(terms)
        at = at * UNROLL
        for u in range(UNROLL):
            terms = [poles[m] * terms[m] for m in range(MODES)]
            sums = terms
            while len(sums) > 1:
                sums = [sums[i] + sums[i + 1] for i in range(0, len(sums), 2)]
            here = pl.ds(pl.multiple_of((at + u) * CHUNKS, CHUNKS), CHUNKS)
            out[pl.ds(at + u, CHUNKS, stride=length), :] = direct[here, :] + first[here, :] * sums[0]
        return tuple(terms)

    terms = tuple(begins[m * CHUNKS : (m + 1) * CHUNKS, :] for m in range(MODES))
    lax.fori_loop(0, length // UNROLL, steps, terms)


def final_part(carried, first, direct, starts, weights, decays):
    rows, width = first.shape
    column = lambda n: pl.BlockSpec((n, LANES), lambda i: (0, i))
    return pl.pallas_call(
        functools.partial(final_kernel, rows // CHUNKS),
        grid=(width // LANES,),
        in_specs=[
            column(MODES),
            column(rows),
            column(rows),
            pl.BlockSpec((CHUNKS, MODES, LANES), lambda i: (0, 0, i)),
            column(MODES),
            column(MODES),
        ],
        out_specs=column(rows),
        out_shape=jax.ShapeDtypeStruct((rows, width), jnp.float32),
        scratch_shapes=[pltpu.VMEM((MODES * CHUNKS, LANES), jnp.float32)],
        compiler_params=pltpu.CompilerParams(vmem_limit_bytes=32 * 2**20),
        cost_estimate=pl.CostEstimate(
            flops=rows * width * 36, bytes_accessed=rows * width * 12, transcendentals=0
        ),
    )(carried, first, direct, starts, weights, decays)


def per_device(tokens, in_weights, short_taps, residues, decays, skip_gain):
    rows = tokens.shape[0]
    blocks = lax.axis_size("ctx")
    mine = lax.axis_index("ctx")
    weights = (residues * jnp.sqrt(2.0 * decays / MODES)).T
    rates = decays.T
    projected = jnp.einsum(
        "td,sdc->stc",
        lax.all_gather(tokens, "ch", axis=1, tiled=True),
        in_weights,
        preferred_element_type=jnp.float32,
    )
    previous = lax.ppermute(
        projected[:, rows - HALO :, :], "ctx", [(i, i + 1) for i in range(blocks - 1)]
    )
    padded = jnp.concatenate([previous, projected], axis=1)
    first, direct, starts, last = local_part(
        padded, short_taps, weights, rates, skip_gain[None, :]
    )
    ahead = jnp.arange(blocks) - mine - 1
    ahead = ahead[:, None, None]
    worth = jnp.where(
        ahead >= 0, jnp.exp(-rates[None] * (rows * jnp.maximum(ahead, 0)).astype(jnp.float32)), 0.0
    )
    arrived = lax.all_to_all(worth * last[None], "ctx", split_axis=0, concat_axis=0, tiled=True)
    return final_part(jnp.sum(arrived, axis=0), first, direct, starts, weights, rates)


def solution(mesh):
    return jax.shard_map(
        per_device,
        mesh=mesh,
        in_specs=(
            P("ctx", "ch"),
            P(None, None, "ch"),
            P(None, None, "ch"),
            P("ch", None),
            P("ch", None),
            P("ch"),
        ),
        out_specs=P("ctx", "ch"),
        check_vma=False,
    )
```

```python
import functools

import jax
import jax.numpy as jnp
import numpy as np
from jax import lax
from jax.experimental import pallas as pl
from jax.experimental.pallas import tpu as pltpu
from jax.sharding import PartitionSpec as P

MODES = 16
TAPS = 7
HALO = 16
CHUNKS = 8
UNROLL = 8
LANES = 128


def wide(row):
    return jnp.broadcast_to(row, (CHUNKS, LANES))


def local_kernel(length, proj, taps, weights, decays, skip, first, direct, starts, last, ends):
    poles = [wide(jnp.exp(-decays[m : m + 1, :])) for m in range(MODES)]
    gains = [wide(weights[m : m + 1, :]) for m in range(MODES)]
    skip_row = wide(skip[0:1, :])

    def steps(at, states):
        states = list(states)
        at = at * UNROLL
        rows = [
            [
                proj[s, pl.ds(at + HALO - (TAPS - 1) + k, CHUNKS, stride=length), :]
                for k in range(UNROLL + TAPS - 1)
            ]
            for s in range(3)
        ]
        coef = [[wide(taps[s, j : j + 1, :]) for j in range(TAPS)] for s in range(3)]
        for u in range(UNROLL):
            filtered = [sum(coef[s][j] * rows[s][u + j] for j in range(TAPS)) for s in range(3)]
            gated = filtered[1] * filtered[2]
            total = skip_row * gated
            for m in range(MODES):
                states[m] = poles[m] * states[m] + gated
                total = total + gains[m] * states[m]
            here = pl.ds(pl.multiple_of((at + u) * CHUNKS, CHUNKS), CHUNKS)
            first[here, :] = filtered[0]
            direct[here, :] = filtered[0] * total
        return tuple(states)

    zero = jnp.zeros((CHUNKS, LANES), jnp.float32)
    states = lax.fori_loop(0, length // UNROLL, steps, (zero,) * MODES)
    for m in range(MODES):
        ends[m * CHUNKS : (m + 1) * CHUNKS, :] = states[m]
    over = jnp.exp(-decays[...] * float(length))
    carry = jnp.zeros((MODES, LANES), jnp.float32)
    for c in range(CHUNKS):
        starts[c] = carry
        carry = over * carry + ends[pl.ds(c, MODES, stride=CHUNKS), :]
    last[...] = carry


def local_part(proj, taps, weights, decays, skip):
    rows = proj.shape[1] - HALO
    width = proj.shape[2]
    flat = jax.ShapeDtypeStruct((rows, width), jnp.float32)
    column = lambda n: pl.BlockSpec((n, LANES), lambda i: (0, i))
    return pl.pallas_call(
        functools.partial(local_kernel, rows // CHUNKS),
        grid=(width // LANES,),
        in_specs=[
            pl.BlockSpec((3, rows + HALO, LANES), lambda i: (0, 0, i)),
            pl.BlockSpec((3, TAPS, LANES), lambda i: (0, 0, i)),
            column(MODES),
            column(MODES),
            column(1),
        ],
        out_specs=[
            column(rows),
            column(rows),
            pl.BlockSpec((CHUNKS, MODES, LANES), lambda i: (0, 0, i)),
            column(MODES),
        ],
        out_shape=[
            flat,
            flat,
            jax.ShapeDtypeStruct((CHUNKS, MODES, width), jnp.float32),
            jax.ShapeDtypeStruct((MODES, width), jnp.float32),
        ],
        scratch_shapes=[pltpu.VMEM((MODES * CHUNKS, LANES), jnp.float32)],
        compiler_params=pltpu.CompilerParams(vmem_limit_bytes=32 * 2**20),
        cost_estimate=pl.CostEstimate(
            flops=rows * width * 110, bytes_accessed=rows * width * 20, transcendentals=0
        ),
    )(proj, taps, weights, decays, skip)


def final_kernel(length, carried, first, direct, starts, weights, decays, out, begins):
    over = jnp.exp(-decays[...] * float(length))
    reach = jnp.ones_like(over)
    for c in range(CHUNKS):
        begins[pl.ds(c, MODES, stride=CHUNKS), :] = weights[...] * (starts[c] + reach * carried[...])
        reach = reach * over
    poles = [wide(jnp.exp(-decays[m : m + 1, :])) for m in range(MODES)]

    def steps(at, terms):
        terms = list(terms)
        at = at * UNROLL
        for u in range(UNROLL):
            terms = [poles[m] * terms[m] for m in range(MODES)]
            sums = terms
            while len(sums) > 1:
                sums = [sums[i] + sums[i + 1] for i in range(0, len(sums), 2)]
            here = pl.ds(pl.multiple_of((at + u) * CHUNKS, CHUNKS), CHUNKS)
            out[pl.ds(at + u, CHUNKS, stride=length), :] = direct[here, :] + first[here, :] * sums[0]
        return tuple(terms)

    terms = tuple(begins[m * CHUNKS : (m + 1) * CHUNKS, :] for m in range(MODES))
    lax.fori_loop(0, length // UNROLL, steps, terms)


def final_part(carried, first, direct, starts, weights, decays):
    rows, width = first.shape
    column = lambda n: pl.BlockSpec((n, LANES), lambda i: (0, i))
    return pl.pallas_call(
        functools.partial(final_kernel, rows // CHUNKS),
        grid=(width // LANES,),
        in_specs=[
            column(MODES),
            column(rows),
            column(rows),
            pl.BlockSpec((CHUNKS, MODES, LANES), lambda i: (0, 0, i)),
            column(MODES),
            column(MODES),
        ],
        out_specs=column(rows),
        out_shape=jax.ShapeDtypeStruct((rows, width), jnp.float32),
        scratch_shapes=[pltpu.VMEM((MODES * CHUNKS, LANES), jnp.float32)],
        compiler_params=pltpu.CompilerParams(vmem_limit_bytes=32 * 2**20),
        cost_estimate=pl.CostEstimate(
            flops=rows * width * 36, bytes_accessed=rows * width * 12, transcendentals=0
        ),
    )(carried, first, direct, starts, weights, decays)


def project_kernel(count, ids, *refs):
    blocks, weights = refs[:count], refs[count : 5 * count]
    sums, out = refs[5 * count : -1], refs[-1]
    total = None
    for b in range(count):
        wide_weights = jnp.concatenate(
            [
                jnp.concatenate([weights[4 * b + z][s] for s in range(3)], axis=1)
                for z in range(4)
            ],
            axis=0,
        )
        part = jnp.dot(blocks[b][...], wide_weights, preferred_element_type=jnp.float32)
        total = part if total is None else total + part
    for s in range(3):
        here = total[:, s * LANES : (s + 1) * LANES]
        out[s] = here + sums[0][s] if sums else here


def project(sums, blocks, ids, at, in_weights):
    rows, depth = blocks[0].shape
    count = len(blocks)
    tile = rows // 5 if rows % 80 == 0 else rows // 3
    piece = lambda k: pl.BlockSpec((3, LANES, LANES), lambda i, ids: (0, ids[4 * at + k], 0))
    total = pl.BlockSpec((3, tile, LANES), lambda i, ids: (0, i, 0))
    extra = [] if sums is None else [sums]
    return pl.pallas_call(
        functools.partial(project_kernel, count),
        grid_spec=pltpu.PrefetchScalarGridSpec(
            num_scalar_prefetch=1,
            grid=(rows // tile,),
            in_specs=[pl.BlockSpec((tile, depth), lambda i, ids: (i, 0))] * count
            + [piece(k) for k in range(4 * count)]
            + [total] * len(extra),
            out_specs=total,
        ),
        out_shape=jax.ShapeDtypeStruct((3, rows, LANES), jnp.float32),
        input_output_aliases={1 + 5 * count: 0} if extra else {},
        compiler_params=pltpu.CompilerParams(vmem_limit_bytes=32 * 2**20),
        cost_estimate=pl.CostEstimate(
            flops=rows * depth * count * 768, bytes_accessed=rows * 3000, transcendentals=0
        ),
    )(ids, *blocks, *[in_weights] * (4 * count), *extra)


def per_device(tokens, in_weights, short_taps, residues, decays, skip_gain):
    rows = tokens.shape[0]
    blocks = lax.axis_size("ctx")
    ring = 8
    lines = lax.axis_size("ch") // ring
    mine = lax.axis_index("ctx")
    weights = (residues * jnp.sqrt(2.0 * decays / MODES)).T
    rates = decays.T

    def beside(block, step):
        return lax.ppermute(
            block, "ch", [(z * ring + y, (z ^ step) * ring + y) for z in range(lines) for y in range(ring)]
        )

    def onward(block, cross):
        route = []
        for i in range(blocks):
            to = i ^ 1 if cross else i
            way = 1 if to % 2 == 0 else -1
            for z in range(lines):
                for y in range(ring):
                    route.append(
                        ((i * lines + z) * ring + y, (to * lines + z) * ring + (y + way) % ring)
                    )
        return lax.ppermute(block, ("ctx", "ch"), route)

    def other_core(block):
        return lax.ppermute(block, "ctx", [(i, i ^ 1) for i in range(blocks)])

    before = lax.ppermute(tokens[rows - HALO :], "ctx", [(i, i + 1) for i in range(blocks - 1)])
    own = jnp.concatenate([before, tokens], axis=0)
    block = jnp.concatenate([own] + [beside(own, k) for k in range(1, lines)], axis=1)
    table = np.zeros((2, lines, ring, ring, lines), np.int32)
    for c, z, y, k in np.ndindex(2, lines, ring, lines):
        way = 1 - 2 * c
        places = [y] + [y + way * d for step in range(1, ring // 2) for d in (-step, step)] + [y + ring // 2]
        table[c, z, y, :, k] = (z ^ k) * ring + np.array(places) % ring
    ids = lax.dynamic_index_in_dim(
        jnp.asarray(table.reshape(2, lines * ring, -1)[np.arange(blocks) % 2].reshape(-1, ring * lines)),
        mine * lines * ring + lax.axis_index("ch"), 0, keepdims=False,
    )
    straight, crossed = onward(block, False), onward(block, True)
    sums, waiting, at = None, [block], 0
    for step in range(1, ring // 2):
        swapped = other_core(crossed)
        here, last_crossed = straight, crossed
        straight = onward(straight, False)
        if step < ring // 2 - 1:
            crossed = onward(crossed, False)
        sums = project(sums, waiting, ids, at, in_weights)
        at += len(waiting)
        waiting = [here, swapped]
        straight, sums = lax.optimization_barrier((straight, sums))
    sums = project(sums, waiting, ids, at, in_weights)
    sums = project(sums, [straight], ids, ring - 1, in_weights)
    first, direct, starts, last = local_part(sums, short_taps, weights, rates, skip_gain[None, :])
    ahead = (jnp.arange(blocks) - mine - 1)[:, None, None]
    worth = jnp.where(
        ahead >= 0, jnp.exp(-rates[None] * (rows * jnp.maximum(ahead, 0)).astype(jnp.float32)), 0.0
    )
    arrived = lax.all_to_all(worth * last[None], "ctx", split_axis=0, concat_axis=0, tiled=True)
    return final_part(jnp.sum(arrived, axis=0), first, direct, starts, weights, rates)


def solution(mesh):
    return jax.shard_map(
        per_device,
        mesh=mesh,
        in_specs=(
            P("ctx", "ch"),
            P(None, None, "ch"),
            P(None, None, "ch"),
            P("ch", None),
            P("ch", None),
            P("ch"),
        ),
        out_specs=P("ctx", "ch"),
        check_vma=False,
    )
```

```python
import functools

import jax
import jax.numpy as jnp
import numpy as np
from jax import lax
from jax.experimental import pallas as pl
from jax.experimental.pallas import tpu as pltpu
from jax.sharding import PartitionSpec as P

MODES = 16
TAPS = 7
HALO = 16
CHUNKS = 8
UNROLL = 8
LANES = 128


def wide(row):
    return jnp.broadcast_to(row, (CHUNKS, LANES))


def local_kernel(length, proj, taps, weights, decays, skip, pack, ends):
    rows = length * CHUNKS
    poles = [wide(jnp.exp(-decays[m : m + 1, :])) for m in range(MODES)]
    gains = [wide(weights[m : m + 1, :]) for m in range(MODES)]
    skip_row = wide(skip[0:1, :])

    def steps(at, states):
        states = list(states)
        at = at * UNROLL
        taken = [
            [
                proj[s, pl.ds(at + HALO - (TAPS - 1) + k, CHUNKS, stride=length), :]
                for k in range(UNROLL + TAPS - 1)
            ]
            for s in range(3)
        ]
        coef = [[wide(taps[s, j : j + 1, :]) for j in range(TAPS)] for s in range(3)]
        for u in range(UNROLL):
            filtered = [sum(coef[s][j] * taken[s][u + j] for j in range(TAPS)) for s in range(3)]
            gated = filtered[1] * filtered[2]
            total = skip_row * gated
            for m in range(MODES):
                states[m] = poles[m] * states[m] + gated
                total = total + gains[m] * states[m]
            here = pl.multiple_of((at + u) * CHUNKS, CHUNKS)
            pack[pl.ds(here, CHUNKS), :] = filtered[0]
            pack[pl.ds(rows + here, CHUNKS), :] = filtered[0] * total
        return tuple(states)

    zero = jnp.zeros((CHUNKS, LANES), jnp.float32)
    states = lax.fori_loop(0, length // UNROLL, steps, (zero,) * MODES)
    for m in range(MODES):
        ends[m * CHUNKS : (m + 1) * CHUNKS, :] = states[m]
    over = jnp.exp(-decays[...] * float(length))
    carry = jnp.zeros((MODES, LANES), jnp.float32)
    for c in range(CHUNKS):
        pack[2 * rows + c * MODES : 2 * rows + (c + 1) * MODES, :] = carry
        carry = over * carry + ends[pl.ds(c, MODES, stride=CHUNKS), :]
    pack[2 * rows + CHUNKS * MODES : 2 * rows + (CHUNKS + 1) * MODES, :] = carry


def local_part(proj, taps, weights, decays, skip):
    rows = proj.shape[1] - HALO
    return pl.pallas_call(
        functools.partial(local_kernel, rows // CHUNKS),
        out_shape=jax.ShapeDtypeStruct((2 * rows + (CHUNKS + 1) * MODES, LANES), jnp.float32),
        scratch_shapes=[pltpu.VMEM((MODES * CHUNKS, LANES), jnp.float32)],
        compiler_params=pltpu.CompilerParams(vmem_limit_bytes=32 * 2**20),
        cost_estimate=pl.CostEstimate(
            flops=rows * LANES * 110, bytes_accessed=rows * LANES * 20, transcendentals=0
        ),
    )(proj, taps, weights, decays, skip)


def final_kernel(rows, half, carried, mine, other, weights, decays, out, begins):
    length = rows // CHUNKS
    low = half[0] == 0
    end = slice(2 * rows + CHUNKS * MODES, 2 * rows + (CHUNKS + 1) * MODES)
    poles = [wide(jnp.exp(-decays[m : m + 1, :])) for m in range(MODES)]
    over = jnp.exp(-decays[...] * float(length))
    beyond = jnp.exp(-decays[...] * float(rows))
    early = carried[...]
    late = beyond * early + jnp.where(low, mine[end, :], other[end, :])
    for pack, begin, offset in (
        (mine, jnp.where(low, early, late), half[0] * rows),
        (other, jnp.where(low, late, early), (1 - half[0]) * rows),
    ):
        reach = jnp.ones_like(over)
        for c in range(CHUNKS):
            start = pack[2 * rows + c * MODES : 2 * rows + (c + 1) * MODES, :]
            begins[pl.ds(c, MODES, stride=CHUNKS), :] = weights[...] * (start + reach * begin)
            reach = reach * over

        def steps(at, terms, pack=pack, offset=offset):
            terms = list(terms)
            at = at * UNROLL
            for u in range(UNROLL):
                terms = [poles[m] * terms[m] for m in range(MODES)]
                sums = terms
                while len(sums) > 1:
                    sums = [sums[i] + sums[i + 1] for i in range(0, len(sums), 2)]
                here = pl.multiple_of((at + u) * CHUNKS, CHUNKS)
                out[pl.ds(offset + at + u, CHUNKS, stride=length), :] = (
                    pack[pl.ds(rows + here, CHUNKS), :] + pack[pl.ds(here, CHUNKS), :] * sums[0]
                )
            return tuple(terms)

        terms = tuple(begins[m * CHUNKS : (m + 1) * CHUNKS, :] for m in range(MODES))
        lax.fori_loop(0, length // UNROLL, steps, terms)


def final_part(half, carried, mine, other, weights, decays):
    rows = (mine.shape[0] - (CHUNKS + 1) * MODES) // 2
    vmem = pl.BlockSpec(memory_space=pltpu.VMEM)
    return pl.pallas_call(
        functools.partial(final_kernel, rows),
        in_specs=[pl.BlockSpec(memory_space=pltpu.SMEM)] + [vmem] * 5,
        out_specs=vmem,
        out_shape=jax.ShapeDtypeStruct((2 * rows, LANES), jnp.float32),
        scratch_shapes=[pltpu.VMEM((MODES * CHUNKS, LANES), jnp.float32)],
        compiler_params=pltpu.CompilerParams(vmem_limit_bytes=32 * 2**20),
        cost_estimate=pl.CostEstimate(
            flops=rows * LANES * 72, bytes_accessed=rows * LANES * 24, transcendentals=0
        ),
    )(half, carried, mine, other, weights, decays)


def project_kernel(count, ids, *refs):
    blocks, weights = refs[:count], refs[count : 5 * count]
    sums, out = refs[5 * count : -1], refs[-1]
    total = None
    for b in range(count):
        wide_weights = jnp.concatenate(
            [
                jnp.concatenate([weights[4 * b + z][s] for s in range(3)], axis=1)
                for z in range(4)
            ],
            axis=0,
        )
        part = jnp.dot(blocks[b][...], wide_weights, preferred_element_type=jnp.float32)
        total = part if total is None else total + part
    for s in range(3):
        here = total[:, s * LANES : (s + 1) * LANES]
        out[s] = here + sums[0][s] if sums else here


def project(sums, blocks, ids, at, in_weights):
    rows, depth = blocks[0].shape
    count = len(blocks)
    tile = rows
    piece = lambda k: pl.BlockSpec((3, LANES, LANES), lambda i, ids: (0, ids[4 * at + k], 0))
    total = pl.BlockSpec((3, tile, LANES), lambda i, ids: (0, i, 0))
    extra = [] if sums is None else [sums]
    return pl.pallas_call(
        functools.partial(project_kernel, count),
        grid_spec=pltpu.PrefetchScalarGridSpec(
            num_scalar_prefetch=1,
            grid=(rows // tile,),
            in_specs=[pl.BlockSpec((tile, depth), lambda i, ids: (i, 0))] * count
            + [piece(k) for k in range(4 * count)]
            + [total] * len(extra),
            out_specs=total,
        ),
        out_shape=jax.ShapeDtypeStruct((3, rows, LANES), jnp.float32),
        input_output_aliases={1 + 5 * count: 0} if extra else {},
        compiler_params=pltpu.CompilerParams(vmem_limit_bytes=32 * 2**20),
        cost_estimate=pl.CostEstimate(
            flops=rows, bytes_accessed=rows, transcendentals=0
        ),
    )(ids, *blocks, *[in_weights] * (4 * count), *extra)


def per_device(tokens, in_weights, short_taps, residues, decays, skip_gain):
    rows = tokens.shape[0]
    part = rows // 2
    blocks = lax.axis_size("ctx")
    ring = 8
    lines = lax.axis_size("ch") // ring
    mine = lax.axis_index("ctx")
    place = mine * lines * ring + lax.axis_index("ch")
    half = lax.axis_index("ch") // ring % 2
    weights = (residues * jnp.sqrt(2.0 * decays / MODES)).T
    rates = decays.T

    def beside(block, step):
        return lax.ppermute(
            block, "ch", [(z * ring + y, (z ^ step) * ring + y) for z in range(lines) for y in range(ring)]
        )

    def onward(block):
        route = []
        for i in range(blocks):
            for z in range(lines):
                for y in range(ring):
                    at = (i * lines + z) * ring
                    route.append((at + y, at + (y + 1 - i % 2 * 2) % ring))
        return lax.ppermute(block, ("ctx", "ch"), route)

    def other_core(block):
        return lax.ppermute(block, "ctx", [(i, i ^ 1) for i in range(blocks)])

    table = np.zeros((2, 2, lines, ring, ring, lines), np.int32)
    for c, z, y, k in np.ndindex(2, lines, ring, lines):
        way = 1 - 2 * c
        places = [y] + [y + way * d for step in range(1, ring // 2) for d in (-step, step)] + [y + ring // 2]
        ids = (z ^ k) * ring + np.array(places) % ring
        count = lines * ring // 2
        table[c, 0, z, y, :, k] = ids
        table[c, 1, z, y, :, k] = ids % count + count * (ids // count != c)
    table = table.transpose(0, 2, 3, 1, 4, 5).reshape(2, lines * ring, -1)[np.arange(blocks) % 2]
    ids = lax.dynamic_index_in_dim(
        jnp.asarray(table.reshape(-1, 2 * lines * ring)), place, 0, keepdims=False
    )

    before = lax.ppermute(tokens[rows - HALO :], "ctx", [(i, i + 1) for i in range(blocks - 1)])
    padded = jnp.concatenate([before, tokens], axis=0)
    kept = lax.dynamic_slice_in_dim(padded, half * part, part + HALO, 0)
    given = lax.dynamic_slice_in_dim(padded, (1 - half) * part, part + HALO, 0)
    block = jnp.concatenate([kept, beside(given, 1), beside(kept, 2), beside(given, 3)], axis=1)
    count = in_weights.shape[1] // 2
    half_weights = lax.dynamic_slice_in_dim(in_weights, mine % 2 * count, count, 1)
    half_weights, block = lax.optimization_barrier((half_weights, block))
    straight = onward(block)
    crossed = onward(other_core(block))
    half_weights = beside(half_weights, 1)

    sums, waiting, at = None, [block], 0
    arrived = [block]
    for step in range(1, ring // 2):
        swapped = other_core(crossed)
        if step == ring // 2 - 1:
            half_weights, straight = lax.optimization_barrier((half_weights, straight))
        here = straight
        straight = onward(straight)
        if step < ring // 2 - 1:
            crossed = onward(crossed)
        sums = project(sums, waiting, ids, at, in_weights)
        at += len(waiting)
        waiting = [here, swapped]
        arrived += waiting
        straight, sums = lax.optimization_barrier((straight, sums))
    their_weights = jnp.concatenate([half_weights, other_core(half_weights)], axis=1)
    sums = project(sums, waiting, ids, at, in_weights)
    theirs = project(None, arrived[:3], ids, ring, their_weights)
    theirs = project(theirs, arrived[3:], ids, ring + 3, their_weights)
    straight, sums, theirs = lax.optimization_barrier((straight, sums, theirs))
    theirs = project(theirs, [straight], ids, 2 * ring - 1, their_weights)
    sums = project(sums, [straight], ids, ring - 1, in_weights)

    own_values = (short_taps, weights, rates, skip_gain[None, :])
    packed = jnp.concatenate([short_taps.reshape(3 * TAPS, -1), weights, rates, skip_gain[None, :]], axis=0)
    packed = beside(packed, 1)
    their_values = (
        packed[: 3 * TAPS].reshape(3, TAPS, -1),
        packed[3 * TAPS : 3 * TAPS + MODES],
        packed[3 * TAPS + MODES : 3 * TAPS + 2 * MODES],
        packed[3 * TAPS + 2 * MODES :],
    )
    their_pack = local_part(theirs, *their_values)
    other = beside(their_pack, 1)
    pack = local_part(sums, *own_values)

    ahead = (jnp.arange(blocks) - mine - 1)[:, None, None]

    def worth(rate, state):
        distance = (rows * jnp.maximum(ahead, 0) + (1 - half) * part).astype(jnp.float32)
        return jnp.where(ahead >= 0, jnp.exp(-rate[None] * distance), 0.0) * state[None]

    to_own = worth(rates, pack[-MODES:])
    to_their = worth(their_values[2], their_pack[-MODES:])
    states = jnp.where(half == 0, jnp.stack([to_own, to_their], 1), jnp.stack([to_their, to_own], 1))
    groups = [
        [(i * lines + z + q) * ring + y for i in range(blocks) for q in range(2)]
        for z in range(0, lines, 2)
        for y in range(ring)
    ]
    states = lax.all_to_all(
        states.reshape(2 * blocks, MODES, LANES), ("ctx", "ch"), 0, 0, axis_index_groups=groups, tiled=True
    )
    return final_part(
        jnp.full((1,), half, jnp.int32), jnp.sum(states, axis=0), pack, other, weights, rates
    )


def solution(mesh):
    return jax.shard_map(
        per_device,
        mesh=mesh,
        in_specs=(
            P("ctx", "ch"),
            P(None, None, "ch"),
            P(None, None, "ch"),
            P("ch", None),
            P("ch", None),
            P("ch"),
        ),
        out_specs=P("ctx", "ch"),
        check_vma=False,
    )
```

```python
import functools

import jax
import jax.numpy as jnp
import numpy as np
from jax import lax
from jax.experimental import pallas as pl
from jax.experimental.pallas import tpu as pltpu
from jax.sharding import PartitionSpec as P

MODES = 16
TAPS = 7
HALO = 16
CHUNKS = 8
UNROLL = 8
LANES = 128
RING = 8
LINES = 4
SMEM = pl.BlockSpec(memory_space=pltpu.SMEM)
VMEM = pl.BlockSpec(memory_space=pltpu.VMEM)


def wide(row):
    return jnp.broadcast_to(row, (CHUNKS, LANES))


def met_rows(weights, s, at):
    count = weights[0].shape[1] // LANES
    parts = [
        w[s, pl.ds(pl.multiple_of(jnp.clip(at - i * count, 0, count - 1) * LANES, LANES), LANES), :]
        for i, w in enumerate(weights)
    ]
    return parts[0] if len(parts) == 1 else jnp.where(at < count, parts[0], parts[1])


def products(blocks, ids, at, weights):
    total = None
    for b, block in enumerate(blocks):
        rows = [ids[LINES * (at + b) + k] for k in range(LINES)]
        met = jnp.concatenate(
            [jnp.concatenate([met_rows(weights, s, r) for s in range(3)], axis=1) for r in rows], axis=0
        )
        part = jnp.dot(block[...], met, preferred_element_type=jnp.float32)
        total = part if total is None else total + part
    return [total[:, s * LANES : (s + 1) * LANES] for s in range(3)]


def project_kernel(count, kinds, at, ids, *refs):
    weights, refs = refs[:kinds], refs[kinds:]
    blocks, sums, out = refs[:count], refs[count:-1], refs[-1]
    for s, part in enumerate(products(blocks, ids, at, weights)):
        out[s] = sums[0][s] + part if sums else part


def project(sums, blocks, ids, at, in_weights):
    extra = [] if sums is None else [sums]
    rows = blocks[0].shape[0]
    return pl.pallas_call(
        functools.partial(project_kernel, len(blocks), len(in_weights), at),
        in_specs=[SMEM] + [VMEM] * (len(in_weights) + len(blocks) + len(extra)),
        out_specs=VMEM,
        out_shape=jax.ShapeDtypeStruct((3, rows, LANES), jnp.float32),
        input_output_aliases={1 + len(in_weights) + len(blocks): 0} if extra else {},
        compiler_params=pltpu.CompilerParams(vmem_limit_bytes=16 * 2**20),
        cost_estimate=pl.CostEstimate(flops=rows, bytes_accessed=rows, transcendentals=0),
    )(ids, *in_weights, *blocks, *extra)


def local_kernel(count, kinds, at, seat, ids, sums, taps, weights, decays, skip, *refs):
    in_weights, blocks, (pack, sent, proj, ends) = refs[:kinds], refs[kinds : kinds + count], refs[-4:]
    rows = proj.shape[1] - HALO
    length = rows // CHUNKS
    for s, part in enumerate(products(blocks, ids, at, in_weights)):
        proj[s] = sums[s] + part
    poles = [wide(jnp.exp(-decays[m : m + 1, :])) for m in range(MODES)]
    gains = [wide(weights[m : m + 1, :]) for m in range(MODES)]
    skip_row = wide(skip[0:1, :])

    def steps(at, states):
        states = list(states)
        at = at * UNROLL
        taken = [
            [
                proj[s, pl.ds(at + HALO - (TAPS - 1) + k, CHUNKS, stride=length), :]
                for k in range(UNROLL + TAPS - 1)
            ]
            for s in range(3)
        ]
        coef = [[wide(taps[s, j : j + 1, :]) for j in range(TAPS)] for s in range(3)]
        for u in range(UNROLL):
            filtered = [sum(coef[s][j] * taken[s][u + j] for j in range(TAPS)) for s in range(3)]
            gated = filtered[1] * filtered[2]
            total = skip_row * gated
            for m in range(MODES):
                states[m] = poles[m] * states[m] + gated
                total = total + gains[m] * states[m]
            here = pl.multiple_of((at + u) * CHUNKS, CHUNKS)
            pack[pl.ds(here, CHUNKS), :] = filtered[0]
            pack[pl.ds(rows + here, CHUNKS), :] = filtered[0] * total
        return tuple(states)

    zero = jnp.zeros((CHUNKS, LANES), jnp.float32)
    states = lax.fori_loop(0, length // UNROLL, steps, (zero,) * MODES)
    for m in range(MODES):
        ends[m * CHUNKS : (m + 1) * CHUNKS, :] = states[m]
    over = jnp.exp(-decays[...] * float(length))
    carry = jnp.zeros((MODES, LANES), jnp.float32)
    for c in range(CHUNKS):
        pack[2 * rows + c * MODES : 2 * rows + (c + 1) * MODES, :] = carry
        carry = over * carry + ends[pl.ds(c, MODES, stride=CHUNKS), :]
    pack[2 * rows + CHUNKS * MODES : 2 * rows + (CHUNKS + 1) * MODES, :] = carry
    mine, half, owner = seat[0], seat[1], seat[2]
    for j in range(sent.shape[1]):
        ahead = j - mine - 1
        distance = (jnp.maximum(ahead, 0) * 2 * rows + (1 - half) * rows).astype(jnp.float32)
        sent[owner, j] = jnp.where(ahead >= 0, jnp.exp(-decays[...] * distance) * carry, 0.0)


def local_part(sent, sums, blocks, seat, ids, at, in_weights, taps, weights, decays, skip, count):
    rows = sums.shape[1] - HALO
    extra = [] if sent is None else [sent]
    return pl.pallas_call(
        functools.partial(local_kernel, len(blocks), len(in_weights), at),
        in_specs=[SMEM] * 2 + [VMEM] * (5 + len(in_weights) + len(blocks) + len(extra)),
        out_specs=[VMEM] * 2,
        out_shape=[
            jax.ShapeDtypeStruct((2 * rows + (CHUNKS + 1) * MODES, LANES), jnp.float32),
            jax.ShapeDtypeStruct((2, count, MODES, LANES), jnp.float32),
        ],
        input_output_aliases={7 + len(in_weights) + len(blocks): 1} if extra else {},
        scratch_shapes=[
            pltpu.VMEM(sums.shape, jnp.float32),
            pltpu.VMEM((MODES * CHUNKS, LANES), jnp.float32),
        ],
        compiler_params=pltpu.CompilerParams(vmem_limit_bytes=16 * 2**20),
        cost_estimate=pl.CostEstimate(
            flops=rows * LANES * 110, bytes_accessed=rows * LANES * 20, transcendentals=0
        ),
    )(seat, ids, sums, taps, weights, decays, skip, *in_weights, *blocks, *extra)


def final_kernel(rows, seat, arrived, mine, other, weights, decays, out, begins):
    length = rows // CHUNKS
    half = seat[1]
    low = half == 0
    end = slice(2 * rows + CHUNKS * MODES, 2 * rows + (CHUNKS + 1) * MODES)
    poles = [wide(jnp.exp(-decays[m : m + 1, :])) for m in range(MODES)]
    over = jnp.exp(-decays[...] * float(length))
    beyond = jnp.exp(-decays[...] * float(rows))
    early = sum(arrived[k] for k in range(arrived.shape[0]))
    late = beyond * early + jnp.where(low, mine[end, :], other[end, :])
    for pack, begin, offset in (
        (mine, jnp.where(low, early, late), half * rows),
        (other, jnp.where(low, late, early), (1 - half) * rows),
    ):
        reach = jnp.ones_like(over)
        for c in range(CHUNKS):
            start = pack[2 * rows + c * MODES : 2 * rows + (c + 1) * MODES, :]
            begins[pl.ds(c, MODES, stride=CHUNKS), :] = weights[...] * (start + reach * begin)
            reach = reach * over

        def steps(at, terms, pack=pack, offset=offset):
            terms = list(terms)
            at = at * UNROLL
            for u in range(UNROLL):
                terms = [poles[m] * terms[m] for m in range(MODES)]
                sums = terms
                while len(sums) > 1:
                    sums = [sums[i] + sums[i + 1] for i in range(0, len(sums), 2)]
                here = pl.multiple_of((at + u) * CHUNKS, CHUNKS)
                out[pl.ds(offset + at + u, CHUNKS, stride=length), :] = (
                    pack[pl.ds(rows + here, CHUNKS), :] + pack[pl.ds(here, CHUNKS), :] * sums[0]
                )
            return tuple(terms)

        terms = tuple(begins[m * CHUNKS : (m + 1) * CHUNKS, :] for m in range(MODES))
        lax.fori_loop(0, length // UNROLL, steps, terms)


def final_part(seat, arrived, mine, other, weights, decays):
    rows = (mine.shape[0] - (CHUNKS + 1) * MODES) // 2
    return pl.pallas_call(
        functools.partial(final_kernel, rows),
        in_specs=[SMEM] + [VMEM] * 5,
        out_specs=VMEM,
        out_shape=jax.ShapeDtypeStruct((2 * rows, LANES), jnp.float32),
        scratch_shapes=[pltpu.VMEM((MODES * CHUNKS, LANES), jnp.float32)],
        compiler_params=pltpu.CompilerParams(vmem_limit_bytes=16 * 2**20),
        cost_estimate=pl.CostEstimate(
            flops=rows * LANES * 72, bytes_accessed=rows * LANES * 24, transcendentals=0
        ),
    )(seat, arrived, mine, other, weights, decays)


def per_device(tokens, in_weights, short_taps, residues, decays, skip_gain):
    rows = tokens.shape[0]
    part = rows // 2
    blocks = lax.axis_size("ctx")
    ring, lines = RING, LINES
    mine = lax.axis_index("ctx")
    place = mine * lines * ring + lax.axis_index("ch")
    half = lax.axis_index("ch") // ring % 2
    weights = (residues * jnp.sqrt(2.0 * decays / MODES)).T
    rates = decays.T

    def beside(block, step):
        return lax.ppermute(
            block, "ch", [(z * ring + y, (z ^ step) * ring + y) for z in range(lines) for y in range(ring)]
        )

    def onward(block):
        route = []
        for i in range(blocks):
            for z in range(lines):
                for y in range(ring):
                    at = (i * lines + z) * ring
                    route.append((at + y, at + (y + 1 - i % 2 * 2) % ring))
        return lax.ppermute(block, ("ctx", "ch"), route)

    def other_core(block):
        return lax.ppermute(block, "ctx", [(i, i ^ 1) for i in range(blocks)])

    table = np.zeros((2, 2, lines, ring, ring, lines), np.int32)
    for c, z, y, k in np.ndindex(2, lines, ring, lines):
        way = 1 - 2 * c
        places = [y] + [y + way * d for step in range(1, ring // 2) for d in (-step, step)] + [y + ring // 2]
        ids = (z ^ k) * ring + np.array(places) % ring
        count = lines * ring // 2
        table[c, 0, z, y, :, k] = ids
        table[c, 1, z, y, :, k] = ids % count + count * (ids // count != c)
    table = table.transpose(0, 2, 3, 1, 4, 5).reshape(2, lines * ring, -1)[np.arange(blocks) % 2]
    ids = lax.dynamic_index_in_dim(
        jnp.asarray(table.reshape(-1, 2 * lines * ring)), place, 0, keepdims=False
    )

    seat = jnp.stack([mine, half, half]).astype(jnp.int32)
    other_seat = jnp.stack([mine, half, 1 - half]).astype(jnp.int32)

    before = lax.ppermute(tokens[rows - HALO :], "ctx", [(i, i + 1) for i in range(blocks - 1)])
    padded = jnp.concatenate([before, tokens], axis=0)
    kept = lax.dynamic_slice_in_dim(padded, half * part, part + HALO, 0)
    given = lax.dynamic_slice_in_dim(padded, (1 - half) * part, part + HALO, 0)
    nearest = beside(given, 1)
    count = in_weights.shape[1] // 2
    half_weights = lax.dynamic_slice_in_dim(in_weights, mine % 2 * count, count, 1)
    values = jnp.concatenate([short_taps.reshape(3 * TAPS, -1), weights, rates, skip_gain[None, :]], axis=0)
    nearest, half_weights, values = lax.optimization_barrier((nearest, half_weights, values))
    half_weights, values = beside(half_weights, 1), beside(values, 1)
    block = jnp.concatenate([kept, nearest, beside(kept, 2), beside(given, 3)], axis=1)

    straight, turned = onward(block), other_core(block)
    crossed = onward(turned)
    sums, waiting, met = None, [block], 0
    arrived = []
    for step in range(1, ring // 2):
        straight, turned = lax.optimization_barrier((straight, turned))
        crossed, here = lax.optimization_barrier((crossed, straight))
        turned = crossed
        if step == ring // 2 - 1:
            crossed, waiting[1] = lax.optimization_barrier((crossed, waiting[1]))
        straight = onward(straight)
        swapped = other_core(crossed)
        if step < ring // 2 - 1:
            crossed = onward(crossed)
        sums = project(sums, waiting, ids, met, [in_weights])
        arrived += waiting
        met += len(waiting)
        waiting = [here, swapped]
        if step < ring // 2 - 1:
            straight, sums = lax.optimization_barrier((straight, sums))
    half_weights, sums = lax.optimization_barrier((half_weights, sums))
    their_weights = [half_weights, other_core(half_weights)]
    theirs = project(None, arrived[:met], ids, ring, their_weights)
    waiting.append(straight)

    other_pack, sent = local_part(
        None, theirs, waiting, other_seat, ids, ring + met, their_weights,
        values[: 3 * TAPS].reshape(3, TAPS, -1),
        values[3 * TAPS : 3 * TAPS + MODES],
        values[3 * TAPS + MODES : 3 * TAPS + 2 * MODES],
        values[3 * TAPS + 2 * MODES :],
        blocks,
    )
    other = beside(other_pack, 1)
    pack, sent = local_part(
        sent, sums, waiting, seat, ids, met, [in_weights], short_taps, weights, rates, skip_gain[None, :], blocks
    )
    groups = [
        [(i * lines + z + q) * ring + y for q in range(2) for i in range(blocks)]
        for z in range(0, lines, 2)
        for y in range(ring)
    ]
    states = lax.all_to_all(
        sent.reshape(2 * blocks, MODES, LANES), ("ctx", "ch"), 0, 0, axis_index_groups=groups, tiled=True
    )
    return final_part(seat, states, pack, other, weights, rates)


def solution(mesh):
    return jax.shard_map(
        per_device,
        mesh=mesh,
        in_specs=(
            P("ctx", "ch"),
            P(None, None, "ch"),
            P(None, None, "ch"),
            P("ch", None),
            P("ch", None),
            P("ch"),
        ),
        out_specs=P("ctx", "ch"),
        check_vma=False,
    )
```

```python
import functools

import jax
import jax.numpy as jnp
import numpy as np
from jax import lax
from jax.experimental import pallas as pl
from jax.experimental.pallas import tpu as pltpu
from jax.sharding import PartitionSpec as P

MODES = 16
TAPS = 7
HALO = 16
CHUNKS = 8
UNROLL = 8
LANES = 128
RING = 8
LINES = 4
SMEM = pl.BlockSpec(memory_space=pltpu.SMEM)
VMEM = pl.BlockSpec(memory_space=pltpu.VMEM)
ANY = pl.BlockSpec(memory_space=pl.ANY)


def after(value, earlier):
    return lax.optimization_barrier((value, earlier))[0]


def wide(row):
    return jnp.broadcast_to(row, (CHUNKS, LANES))


def fetch(count, at, ids, weights, blocks, block_buf, weight_buf, sems):
    pending = []
    for b in range(count):
        here = [pltpu.make_async_copy(blocks[b], block_buf.at[b], sems.at[b, 0])]
        here[0].start()
        for k in range(LINES):
            row = ids[LINES * (at + b) + k]
            for s in range(3):
                target = weight_buf.at[b, k * LANES : (k + 1) * LANES, s * LANES : (s + 1) * LANES]
                sem = sems.at[b, 1 + 3 * k + s]
                most = weights[0].shape[1] // LANES
                copies = [
                    pltpu.make_async_copy(
                        w.at[s, pl.ds(pl.multiple_of(jnp.clip(row - i * most, 0, most - 1) * LANES, LANES), LANES), :],
                        target, sem,
                    )
                    for i, w in enumerate(weights)
                ]
                if len(copies) == 1:
                    copies[0].start()
                else:
                    pl.when(row < most)(copies[0].start)
                    pl.when(row >= most)(copies[1].start)
                here.append(copies[0])
        pending.append(here)
    return pending


def products(pending, block_buf, weight_buf):
    total = None
    for b, copies in enumerate(pending):
        for copy in copies:
            copy.wait()
        part = jnp.dot(block_buf[b], weight_buf[b], preferred_element_type=jnp.float32)
        total = part if total is None else total + part
    return [total[:, s * LANES : (s + 1) * LANES] for s in range(3)]


def buffers(blocks):
    count, (rows, depth) = len(blocks), blocks[0].shape
    return [
        pltpu.VMEM((count, rows, depth), jnp.bfloat16),
        pltpu.VMEM((count, depth, 3 * LANES), jnp.bfloat16),
        pltpu.SemaphoreType.DMA((count, 1 + 3 * LINES)),
    ]


def project_kernel(count, kinds, at, ids, *refs):
    weights, blocks, refs = refs[:kinds], refs[kinds : kinds + count], refs[kinds + count :]
    sums, out, (block_buf, weight_buf, sems) = refs[:-4], refs[-4], refs[-3:]
    pending = fetch(count, at, ids, weights, blocks, block_buf, weight_buf, sems)
    for s, part in enumerate(products(pending, block_buf, weight_buf)):
        out[s] = sums[0][s] + part if sums else part


def project(sums, blocks, ids, at, in_weights):
    extra = [] if sums is None else [sums]
    rows = blocks[0].shape[0]
    return pl.pallas_call(
        functools.partial(project_kernel, len(blocks), len(in_weights), at),
        in_specs=[SMEM] + [ANY] * (len(in_weights) + len(blocks)) + [VMEM] * len(extra),
        out_specs=VMEM,
        scratch_shapes=buffers(blocks),
        out_shape=jax.ShapeDtypeStruct((3, rows, LANES), jnp.float32),
        input_output_aliases={1 + len(in_weights) + len(blocks): 0} if extra else {},
        compiler_params=pltpu.CompilerParams(vmem_limit_bytes=16 * 2**20),
        cost_estimate=pl.CostEstimate(flops=rows, bytes_accessed=rows, transcendentals=0),
    )(ids, *in_weights, *blocks, *extra)


def local_kernel(count, kinds, at, seat, ids, sums, taps, weights, decays, skip, *refs):
    in_weights, blocks = refs[:kinds], refs[kinds : kinds + count]
    pack, sent, proj, ends, block_buf, weight_buf, sems = refs[-7:]
    pending = fetch(count, at, ids, in_weights, blocks, block_buf, weight_buf, sems)
    rows = sums.shape[1] - HALO
    length = rows // CHUNKS
    early = TAPS - 1
    top = lax.broadcasted_iota(jnp.int32, (CHUNKS, LANES), 0) == 0
    for s, part in enumerate(products(pending, block_buf, weight_buf)):
        proj[s, early * CHUNKS :, :] = sums[s, HALO:, :] + part[HALO:]
        halo = sums[s, :HALO, :] + part[:HALO]
        for p in range(early):
            end = pltpu.roll(proj[s, (length + p) * CHUNKS : (length + p + 1) * CHUNKS, :], 1, 0)
            proj[s, p * CHUNKS : (p + 1) * CHUNKS, :] = jnp.where(top, wide(halo[HALO - early + p : HALO - early + p + 1]), end)
    poles = [wide(jnp.exp(-decays[m : m + 1, :])) for m in range(MODES)]
    gains = [wide(weights[m : m + 1, :]) for m in range(MODES)]
    skip_row = wide(skip[0:1, :])

    def steps(at, states):
        states = list(states)
        at = at * UNROLL
        taken = [
            [
                proj[s, pl.ds(pl.multiple_of((at + k) * CHUNKS, CHUNKS), CHUNKS), :]
                for k in range(UNROLL + TAPS - 1)
            ]
            for s in range(3)
        ]
        coef = [[wide(taps[s, j : j + 1, :]) for j in range(TAPS)] for s in range(3)]
        for u in range(UNROLL):
            filtered = [sum(coef[s][j] * taken[s][u + j] for j in range(TAPS)) for s in range(3)]
            gated = filtered[1] * filtered[2]
            total = skip_row * gated
            for m in range(MODES):
                states[m] = poles[m] * states[m] + gated
                total = total + gains[m] * states[m]
            here = pl.multiple_of((at + u) * CHUNKS, CHUNKS)
            pack[pl.ds(here, CHUNKS), :] = filtered[0]
            pack[pl.ds(rows + here, CHUNKS), :] = filtered[0] * total
        return tuple(states)

    zero = jnp.zeros((CHUNKS, LANES), jnp.float32)
    states = lax.fori_loop(0, length // UNROLL, steps, (zero,) * MODES)
    for m in range(MODES):
        ends[m * CHUNKS : (m + 1) * CHUNKS, :] = states[m]
    over = jnp.exp(-decays[...] * float(length))
    carry = jnp.zeros((MODES, LANES), jnp.float32)
    for c in range(CHUNKS):
        pack[2 * rows + c * MODES : 2 * rows + (c + 1) * MODES, :] = carry
        carry = over * carry + ends[pl.ds(c, MODES, stride=CHUNKS), :]
    pack[2 * rows + CHUNKS * MODES : 2 * rows + (CHUNKS + 1) * MODES, :] = carry
    mine, half, owner = seat[0], seat[1], seat[2]
    for j in range(sent.shape[1]):
        ahead = j - mine - 1
        distance = (jnp.maximum(ahead, 0) * 2 * rows + (1 - half) * rows).astype(jnp.float32)
        sent[owner, j] = jnp.where(ahead >= 0, jnp.exp(-decays[...] * distance) * carry, 0.0)


def local_part(sent, sums, blocks, seat, ids, at, in_weights, taps, weights, decays, skip, count):
    rows = sums.shape[1] - HALO
    extra = [] if sent is None else [sent]
    return pl.pallas_call(
        functools.partial(local_kernel, len(blocks), len(in_weights), at),
        in_specs=[SMEM] * 2 + [VMEM] * 5 + [ANY] * (len(in_weights) + len(blocks)) + [VMEM] * len(extra),
        out_specs=[VMEM] * 2,
        out_shape=[
            jax.ShapeDtypeStruct((2 * rows + (CHUNKS + 1) * MODES, LANES), jnp.float32),
            jax.ShapeDtypeStruct((2, count, MODES, LANES), jnp.float32),
        ],
        input_output_aliases={7 + len(in_weights) + len(blocks): 1} if extra else {},
        scratch_shapes=[
            pltpu.VMEM((3, rows + (TAPS - 1) * CHUNKS, LANES), jnp.float32),
            pltpu.VMEM((MODES * CHUNKS, LANES), jnp.float32),
        ]
        + buffers(blocks),
        compiler_params=pltpu.CompilerParams(vmem_limit_bytes=16 * 2**20),
        cost_estimate=pl.CostEstimate(
            flops=rows * LANES * 110, bytes_accessed=rows * LANES * 20, transcendentals=0
        ),
    )(seat, ids, sums, taps, weights, decays, skip, *in_weights, *blocks, *extra)


def final_kernel(rows, seat, arrived, mine, other, weights, decays, out, begins):
    length = rows // CHUNKS
    half = seat[1]
    low = half == 0
    end = slice(2 * rows + CHUNKS * MODES, 2 * rows + (CHUNKS + 1) * MODES)
    poles = [wide(jnp.exp(-decays[m : m + 1, :])) for m in range(MODES)]
    over = jnp.exp(-decays[...] * float(length))
    beyond = jnp.exp(-decays[...] * float(rows))
    early = sum(arrived[k] for k in range(arrived.shape[0]))
    late = beyond * early + jnp.where(low, mine[end, :], other[end, :])
    for pack, begin, offset in (
        (mine, jnp.where(low, early, late), half * rows),
        (other, jnp.where(low, late, early), (1 - half) * rows),
    ):
        reach = jnp.ones_like(over)
        for c in range(CHUNKS):
            start = pack[2 * rows + c * MODES : 2 * rows + (c + 1) * MODES, :]
            begins[pl.ds(c, MODES, stride=CHUNKS), :] = weights[...] * (start + reach * begin)
            reach = reach * over

        def steps(at, terms, pack=pack, offset=offset):
            terms = list(terms)
            at = at * UNROLL
            for u in range(UNROLL):
                terms = [poles[m] * terms[m] for m in range(MODES)]
                sums = terms
                while len(sums) > 1:
                    sums = [sums[i] + sums[i + 1] for i in range(0, len(sums), 2)]
                here = pl.multiple_of((at + u) * CHUNKS, CHUNKS)
                out[pl.ds(offset + at + u, CHUNKS, stride=length), :] = (
                    pack[pl.ds(rows + here, CHUNKS), :] + pack[pl.ds(here, CHUNKS), :] * sums[0]
                )
            return tuple(terms)

        terms = tuple(begins[m * CHUNKS : (m + 1) * CHUNKS, :] for m in range(MODES))
        lax.fori_loop(0, length // UNROLL, steps, terms)


def final_part(seat, arrived, mine, other, weights, decays):
    rows = (mine.shape[0] - (CHUNKS + 1) * MODES) // 2
    return pl.pallas_call(
        functools.partial(final_kernel, rows),
        in_specs=[SMEM] + [VMEM] * 5,
        out_specs=VMEM,
        out_shape=jax.ShapeDtypeStruct((2 * rows, LANES), jnp.float32),
        scratch_shapes=[pltpu.VMEM((MODES * CHUNKS, LANES), jnp.float32)],
        compiler_params=pltpu.CompilerParams(vmem_limit_bytes=16 * 2**20),
        cost_estimate=pl.CostEstimate(
            flops=rows * LANES * 72, bytes_accessed=rows * LANES * 24, transcendentals=0
        ),
    )(seat, arrived, mine, other, weights, decays)


def per_device(tokens, in_weights, short_taps, residues, decays, skip_gain):
    rows = tokens.shape[0]
    part = rows // 2
    blocks = lax.axis_size("ctx")
    ring, lines = RING, LINES
    mine = lax.axis_index("ctx")
    place = mine * lines * ring + lax.axis_index("ch")
    half = lax.axis_index("ch") // ring % 2
    weights = (residues * jnp.sqrt(2.0 * decays / MODES)).T
    rates = decays.T

    def beside(block, step):
        return lax.ppermute(
            block, "ch", [(z * ring + y, (z ^ step) * ring + y) for z in range(lines) for y in range(ring)]
        )

    def onward(block):
        route = []
        for i in range(blocks):
            for z in range(lines):
                for y in range(ring):
                    at = (i * lines + z) * ring
                    route.append((at + y, at + (y + 1 - i % 2 * 2) % ring))
        return lax.ppermute(block, ("ctx", "ch"), route)

    def other_core(block):
        return lax.ppermute(block, "ctx", [(i, i ^ 1) for i in range(blocks)])

    table = np.zeros((2, 2, lines, ring, ring, lines), np.int32)
    for c, z, y, k in np.ndindex(2, lines, ring, lines):
        way = 1 - 2 * c
        places = [y] + [y + way * d for step in range(1, ring // 2) for d in (-step, step)] + [y + ring // 2]
        ids = (z ^ k) * ring + np.array(places) % ring
        count = lines * ring // 2
        table[c, 0, z, y, :, k] = ids
        table[c, 1, z, y, :, k] = ids % count + count * (ids // count != c)
    table = table.transpose(0, 2, 3, 1, 4, 5).reshape(2, lines * ring, -1)[np.arange(blocks) % 2]
    ids = lax.dynamic_index_in_dim(
        jnp.asarray(table.reshape(-1, 2 * lines * ring)), place, 0, keepdims=False
    )

    seat = jnp.stack([mine, half, half]).astype(jnp.int32)
    other_seat = jnp.stack([mine, half, 1 - half]).astype(jnp.int32)

    values = jnp.concatenate([short_taps.reshape(3 * TAPS, -1), weights, rates, skip_gain[None, :]], axis=0)
    values = beside(values, 1)
    before = lax.ppermute(tokens[rows - HALO :], "ctx", [(i, i + 1) for i in range(blocks - 1)])
    ordered = tokens.reshape(2, CHUNKS, part // CHUNKS, -1).swapaxes(1, 2).reshape(2, part, -1)
    before = after(before, values)
    between = tokens[part - HALO : part]
    low = half == 0
    kept = jnp.concatenate([jnp.where(low, before, between), jnp.where(low, ordered[0], ordered[1])], axis=0)
    given = jnp.concatenate([jnp.where(low, between, before), jnp.where(low, ordered[1], ordered[0])], axis=0)
    nearest = beside(given, 1)
    count = in_weights.shape[1] // 2
    half_weights = lax.dynamic_slice_in_dim(in_weights, mine % 2 * count, count, 1)
    half_weights = beside(after(half_weights, nearest), 1)
    block = jnp.concatenate([kept, nearest, beside(kept, 2), beside(given, 3)], axis=1)

    straight, turned = onward(block), other_core(block)
    crossed = onward(turned)
    sums, waiting, met = None, [block], 0
    arrived = []
    for step in range(1, ring // 2):
        straight, turned = lax.optimization_barrier((straight, turned))
        crossed, here = lax.optimization_barrier((crossed, straight))
        turned = crossed
        if step == ring // 2 - 1:
            crossed, waiting[1] = lax.optimization_barrier((crossed, waiting[1]))
        straight = onward(straight)
        swapped = other_core(crossed)
        if step < ring // 2 - 1:
            crossed = onward(crossed)
        sums = project(sums, waiting, ids, met, [in_weights])
        arrived += waiting
        met += len(waiting)
        waiting = [here, swapped]
        if step < ring // 2 - 1:
            straight, sums = lax.optimization_barrier((straight, sums))
    half_weights = after(half_weights, sums)
    their_weights = [half_weights, other_core(half_weights)]
    theirs = project(None, arrived[:met], ids, ring, their_weights)
    waiting.append(straight)

    other_pack, sent = local_part(
        None, theirs, waiting, other_seat, ids, ring + met, their_weights,
        values[: 3 * TAPS].reshape(3, TAPS, -1),
        values[3 * TAPS : 3 * TAPS + MODES],
        values[3 * TAPS + MODES : 3 * TAPS + 2 * MODES],
        values[3 * TAPS + 2 * MODES :],
        blocks,
    )
    other = beside(other_pack, 1)
    pack, sent = local_part(
        sent, sums, waiting, seat, ids, met, [in_weights], short_taps, weights, rates, skip_gain[None, :], blocks
    )
    groups = [
        [(i * lines + z + q) * ring + y for q in range(2) for i in range(blocks)]
        for z in range(0, lines, 2)
        for y in range(ring)
    ]
    states = lax.all_to_all(
        sent.reshape(2 * blocks, MODES, LANES), ("ctx", "ch"), 0, 0, axis_index_groups=groups, tiled=True
    )
    return final_part(seat, states, pack, other, weights, rates)


def solution(mesh):
    return jax.shard_map(
        per_device,
        mesh=mesh,
        in_specs=(
            P("ctx", "ch"),
            P(None, None, "ch"),
            P(None, None, "ch"),
            P("ch", None),
            P("ch", None),
            P("ch"),
        ),
        out_specs=P("ctx", "ch"),
        check_vma=False,
    )
```

```python
import functools

import jax
import jax.numpy as jnp
import numpy as np
from jax import lax
from jax.experimental import pallas as pl
from jax.experimental.pallas import tpu as pltpu
from jax.sharding import PartitionSpec as P

MODES = 16
TAPS = 7
HALO = 16
CHUNKS = 8
UNROLL = 8
LANES = 128
RING = 8
LINES = 4
SMEM = pl.BlockSpec(memory_space=pltpu.SMEM)
VMEM = pl.BlockSpec(memory_space=pltpu.VMEM)


def after(value, earlier):
    return lax.optimization_barrier((value, earlier))[0]


def wide(row):
    return jnp.broadcast_to(row, (CHUNKS, LANES))


def met_rows(weights, s, at):
    count = weights[0].shape[1] // LANES
    parts = [
        w[s, pl.ds(pl.multiple_of(jnp.clip(at - i * count, 0, count - 1) * LANES, LANES), LANES), :]
        for i, w in enumerate(weights)
    ]
    return parts[0] if len(parts) == 1 else jnp.where(at < count, parts[0], parts[1])


def products(blocks, ids, at, weights):
    total = None
    for b, block in enumerate(blocks):
        rows = [ids[LINES * (at + b) + k] for k in range(LINES)]
        met = jnp.concatenate(
            [jnp.concatenate([met_rows(weights, s, r) for s in range(3)], axis=1) for r in rows], axis=0
        )
        part = jnp.dot(block[...], met, preferred_element_type=jnp.float32)
        total = part if total is None else total + part
    return [total[:, s * LANES : (s + 1) * LANES] for s in range(3)]


def project_kernel(count, kinds, at, ids, *refs):
    weights, refs = refs[:kinds], refs[kinds:]
    blocks, sums, out = refs[:count], refs[count:-1], refs[-1]
    for s, part in enumerate(products(blocks, ids, at, weights)):
        out[s] = sums[0][s] + part if sums else part


def project(sums, blocks, ids, at, in_weights):
    extra = [] if sums is None else [sums]
    rows = blocks[0].shape[0]
    return pl.pallas_call(
        functools.partial(project_kernel, len(blocks), len(in_weights), at),
        in_specs=[SMEM] + [VMEM] * (len(in_weights) + len(blocks) + len(extra)),
        out_specs=VMEM,
        out_shape=jax.ShapeDtypeStruct((3, rows, LANES), jnp.float32),
        input_output_aliases={1 + len(in_weights) + len(blocks): 0} if extra else {},
        compiler_params=pltpu.CompilerParams(vmem_limit_bytes=16 * 2**20),
        cost_estimate=pl.CostEstimate(flops=rows, bytes_accessed=rows, transcendentals=0),
    )(ids, *in_weights, *blocks, *extra)


def local_kernel(count, kinds, summed, at, seat, ids, taps, weights, decays, skip, *refs):
    sums, refs = refs[:summed], refs[summed:]
    in_weights, blocks, (pack, sent, proj, ends) = refs[:kinds], refs[kinds : kinds + count], refs[-4:]
    rows = blocks[0].shape[0] - HALO
    length = rows // CHUNKS
    early = TAPS - 1
    top = lax.broadcasted_iota(jnp.int32, (CHUNKS, LANES), 0) == 0
    for s, part in enumerate(products(blocks, ids, at, in_weights)):
        total = sums[0][s] + part if sums else part
        proj[s, early * CHUNKS :, :] = total[HALO:]
        for p in range(early):
            end = pltpu.roll(proj[s, (length + p) * CHUNKS : (length + p + 1) * CHUNKS, :], 1, 0)
            proj[s, p * CHUNKS : (p + 1) * CHUNKS, :] = jnp.where(
                top, wide(total[HALO - early + p : HALO - early + p + 1]), end
            )
    poles = [wide(jnp.exp(-decays[m : m + 1, :])) for m in range(MODES)]
    gains = [wide(weights[m : m + 1, :]) for m in range(MODES)]
    skip_row = wide(skip[0:1, :])

    def steps(at, states):
        states = list(states)
        at = at * UNROLL
        taken = [
            [
                proj[s, pl.ds(pl.multiple_of((at + k) * CHUNKS, CHUNKS), CHUNKS), :]
                for k in range(UNROLL + TAPS - 1)
            ]
            for s in range(3)
        ]
        coef = [[wide(taps[s, j : j + 1, :]) for j in range(TAPS)] for s in range(3)]
        for u in range(UNROLL):
            filtered = [sum(coef[s][j] * taken[s][u + j] for j in range(TAPS)) for s in range(3)]
            gated = filtered[1] * filtered[2]
            total = skip_row * gated
            for m in range(MODES):
                states[m] = poles[m] * states[m] + gated
                total = total + gains[m] * states[m]
            here = pl.multiple_of((at + u) * CHUNKS, CHUNKS)
            pack[pl.ds(here, CHUNKS), :] = filtered[0]
            pack[pl.ds(rows + here, CHUNKS), :] = filtered[0] * total
        return tuple(states)

    zero = jnp.zeros((CHUNKS, LANES), jnp.float32)
    states = lax.fori_loop(0, length // UNROLL, steps, (zero,) * MODES)
    for m in range(MODES):
        ends[m * CHUNKS : (m + 1) * CHUNKS, :] = states[m]
    over = jnp.exp(-decays[...] * float(length))
    carry = jnp.zeros((MODES, LANES), jnp.float32)
    for c in range(CHUNKS):
        pack[2 * rows + c * MODES : 2 * rows + (c + 1) * MODES, :] = carry
        carry = over * carry + ends[pl.ds(c, MODES, stride=CHUNKS), :]
    pack[2 * rows + CHUNKS * MODES : 2 * rows + (CHUNKS + 1) * MODES, :] = carry
    mine, half, owner = seat[0], seat[1], seat[2]
    for j in range(sent.shape[1]):
        ahead = j - mine - 1
        distance = (jnp.maximum(ahead, 0) * 2 * rows + (1 - half) * rows).astype(jnp.float32)
        sent[owner, j] = jnp.where(ahead >= 0, jnp.exp(-decays[...] * distance) * carry, 0.0)


def local_part(sent, sums, blocks, seat, ids, at, in_weights, taps, weights, decays, skip, count):
    rows = blocks[0].shape[0] - HALO
    extra = [] if sent is None else [sent]
    summed = [] if sums is None else [sums]
    return pl.pallas_call(
        functools.partial(local_kernel, len(blocks), len(in_weights), len(summed), at),
        in_specs=[SMEM] * 2 + [VMEM] * (4 + len(summed) + len(in_weights) + len(blocks) + len(extra)),
        out_specs=[VMEM] * 2,
        out_shape=[
            jax.ShapeDtypeStruct((2 * rows + (CHUNKS + 1) * MODES, LANES), jnp.float32),
            jax.ShapeDtypeStruct((2, count, MODES, LANES), jnp.float32),
        ],
        input_output_aliases={6 + len(summed) + len(in_weights) + len(blocks): 1} if extra else {},
        scratch_shapes=[
            pltpu.VMEM((3, rows + (TAPS - 1) * CHUNKS, LANES), jnp.float32),
            pltpu.VMEM((MODES * CHUNKS, LANES), jnp.float32),
        ],
        compiler_params=pltpu.CompilerParams(vmem_limit_bytes=16 * 2**20),
        cost_estimate=pl.CostEstimate(
            flops=rows * LANES * 110, bytes_accessed=rows * LANES * 20, transcendentals=0
        ),
    )(seat, ids, taps, weights, decays, skip, *summed, *in_weights, *blocks, *extra)


def final_kernel(rows, seat, arrived, mine, other, weights, decays, out, begins):
    length = rows // CHUNKS
    half = seat[1]
    low = half == 0
    end = slice(2 * rows + CHUNKS * MODES, 2 * rows + (CHUNKS + 1) * MODES)
    poles = [wide(jnp.exp(-decays[m : m + 1, :])) for m in range(MODES)]
    over = jnp.exp(-decays[...] * float(length))
    beyond = jnp.exp(-decays[...] * float(rows))
    early = sum(arrived[k] for k in range(arrived.shape[0]))
    late = beyond * early + jnp.where(low, mine[end, :], other[end, :])
    for pack, begin, offset in (
        (mine, jnp.where(low, early, late), half * rows),
        (other, jnp.where(low, late, early), (1 - half) * rows),
    ):
        reach = jnp.ones_like(over)
        for c in range(CHUNKS):
            start = pack[2 * rows + c * MODES : 2 * rows + (c + 1) * MODES, :]
            begins[pl.ds(c, MODES, stride=CHUNKS), :] = weights[...] * (start + reach * begin)
            reach = reach * over

        def steps(at, terms, pack=pack, offset=offset):
            terms = list(terms)
            at = at * UNROLL
            for u in range(UNROLL):
                terms = [poles[m] * terms[m] for m in range(MODES)]
                sums = terms
                while len(sums) > 1:
                    sums = [sums[i] + sums[i + 1] for i in range(0, len(sums), 2)]
                here = pl.multiple_of((at + u) * CHUNKS, CHUNKS)
                out[pl.ds(offset + at + u, CHUNKS, stride=length), :] = (
                    pack[pl.ds(rows + here, CHUNKS), :] + pack[pl.ds(here, CHUNKS), :] * sums[0]
                )
            return tuple(terms)

        terms = tuple(begins[m * CHUNKS : (m + 1) * CHUNKS, :] for m in range(MODES))
        lax.fori_loop(0, length // UNROLL, steps, terms)


def final_part(seat, arrived, mine, other, weights, decays):
    rows = (mine.shape[0] - (CHUNKS + 1) * MODES) // 2
    return pl.pallas_call(
        functools.partial(final_kernel, rows),
        in_specs=[SMEM] + [VMEM] * 5,
        out_specs=VMEM,
        out_shape=jax.ShapeDtypeStruct((2 * rows, LANES), jnp.float32),
        scratch_shapes=[pltpu.VMEM((MODES * CHUNKS, LANES), jnp.float32)],
        compiler_params=pltpu.CompilerParams(vmem_limit_bytes=16 * 2**20),
        cost_estimate=pl.CostEstimate(
            flops=rows * LANES * 72, bytes_accessed=rows * LANES * 24, transcendentals=0
        ),
    )(seat, arrived, mine, other, weights, decays)


def per_device(tokens, in_weights, short_taps, residues, decays, skip_gain):
    rows = tokens.shape[0]
    part = rows // 2
    blocks = lax.axis_size("ctx")
    ring, lines = RING, LINES
    mine = lax.axis_index("ctx")
    place = mine * lines * ring + lax.axis_index("ch")
    half = lax.axis_index("ch") // ring % 2
    weights = (residues * jnp.sqrt(2.0 * decays / MODES)).T
    rates = decays.T

    def beside(block, step):
        return lax.ppermute(
            block, "ch", [(z * ring + y, (z ^ step) * ring + y) for z in range(lines) for y in range(ring)]
        )

    def onward(block):
        route = []
        for i in range(blocks):
            for z in range(lines):
                for y in range(ring):
                    at = (i * lines + z) * ring
                    route.append((at + y, at + (y + 1 - i % 2 * 2) % ring))
        return lax.ppermute(block, ("ctx", "ch"), route)

    def other_core(block):
        return lax.ppermute(block, "ctx", [(i, i ^ 1) for i in range(blocks)])

    table = np.zeros((2, 2, lines, ring, ring, lines), np.int32)
    for c, z, y, k in np.ndindex(2, lines, ring, lines):
        way = 1 - 2 * c
        places = [y] + [y + way * d for step in range(1, ring // 2) for d in (-step, step)] + [y + ring // 2]
        ids = (z ^ k) * ring + np.array(places) % ring
        count = lines * ring // 2
        table[c, 0, z, y, :, k] = ids
        table[c, 1, z, y, :, k] = ids % count + count * (ids // count != c)
    table = table.transpose(0, 2, 3, 1, 4, 5).reshape(2, lines * ring, -1)[np.arange(blocks) % 2]
    ids = lax.dynamic_index_in_dim(
        jnp.asarray(table.reshape(-1, 2 * lines * ring)), place, 0, keepdims=False
    )

    seat = jnp.stack([mine, half, half]).astype(jnp.int32)
    other_seat = jnp.stack([mine, half, 1 - half]).astype(jnp.int32)

    before = lax.ppermute(tokens[rows - HALO :], "ctx", [(i, i + 1) for i in range(blocks - 1)])
    ordered = tokens.reshape(2, CHUNKS, part // CHUNKS, -1).swapaxes(1, 2).reshape(2, part, -1)
    between = tokens[part - HALO : part]
    low = half == 0
    kept = jnp.concatenate([jnp.where(low, before, between), jnp.where(low, ordered[0], ordered[1])], axis=0)
    given = jnp.concatenate([jnp.where(low, between, before), jnp.where(low, ordered[1], ordered[0])], axis=0)
    nearest = beside(given, 1)
    count = in_weights.shape[1] // 2
    half_weights = lax.dynamic_slice_in_dim(in_weights, mine % 2 * count, count, 1)
    values = jnp.concatenate([short_taps.reshape(3 * TAPS, -1), weights, rates, skip_gain[None, :]], axis=0)
    half_weights, values = beside(after(half_weights, nearest), 1), beside(values, 1)
    block = jnp.concatenate([kept, nearest, beside(kept, 2), beside(given, 3)], axis=1)

    block = after(block, values)
    straight, turned = onward(block), other_core(block)
    crossed = onward(turned)
    sums, waiting, met = None, [block], 0
    arrived = []
    for step in range(1, ring // 2):
        straight, turned = lax.optimization_barrier((straight, turned))
        crossed, here = lax.optimization_barrier((crossed, straight))
        turned = crossed
        if step == ring // 2 - 1:
            crossed = after(after(crossed, waiting[1]), half_weights)
        straight = onward(straight)
        swapped = other_core(crossed)
        if step < ring // 2 - 1:
            crossed = onward(crossed)
        sums = project(sums, waiting, ids, met, [in_weights])
        arrived += waiting
        met += len(waiting)
        waiting = [here, swapped]
        if step < ring // 2 - 1:
            straight, sums = lax.optimization_barrier((straight, sums))
    half_weights = after(after(half_weights, straight), swapped)
    their_weights = [half_weights, other_core(half_weights)]
    waiting.append(straight)
    pack, sent = local_part(
        None, sums, waiting, seat, ids, met, [in_weights], short_taps, weights, rates, skip_gain[None, :], blocks
    )
    other_pack, sent = local_part(
        sent, None, arrived + waiting, other_seat, ids, ring, their_weights,
        values[: 3 * TAPS].reshape(3, TAPS, -1),
        values[3 * TAPS : 3 * TAPS + MODES],
        values[3 * TAPS + MODES : 3 * TAPS + 2 * MODES],
        values[3 * TAPS + 2 * MODES :],
        blocks,
    )
    other = beside(other_pack, 1)
    groups = [
        [(i * lines + z + q) * ring + y for q in range(2) for i in range(blocks)]
        for z in range(0, lines, 2)
        for y in range(ring)
    ]
    states = lax.all_to_all(
        sent.reshape(2 * blocks, MODES, LANES), ("ctx", "ch"), 0, 0, axis_index_groups=groups, tiled=True
    )
    return final_part(seat, states, pack, other, weights, rates)


def solution(mesh):
    return jax.shard_map(
        per_device,
        mesh=mesh,
        in_specs=(
            P("ctx", "ch"),
            P(None, None, "ch"),
            P(None, None, "ch"),
            P("ch", None),
            P("ch", None),
            P("ch"),
        ),
        out_specs=P("ctx", "ch"),
        check_vma=False,
    )
```

```python
import functools

import jax
import jax.numpy as jnp
import numpy as np
from jax import lax
from jax.experimental import pallas as pl
from jax.experimental.pallas import tpu as pltpu
from jax.sharding import PartitionSpec as P

MODES = 16
TAPS = 7
HALO = 16
CHUNKS = 8
UNROLL = 8
LANES = 128
RING = 8
LINES = 4
SMEM = pl.BlockSpec(memory_space=pltpu.SMEM)
VMEM = pl.BlockSpec(memory_space=pltpu.VMEM)


def after(value, earlier):
    return lax.optimization_barrier((value, earlier))[0]


def wide(row):
    return jnp.broadcast_to(row, (CHUNKS, LANES))


def met_rows(weights, s, at):
    count = weights[0].shape[1] // LANES
    parts = [
        w[s, pl.ds(pl.multiple_of(jnp.clip(at - i * count, 0, count - 1) * LANES, LANES), LANES), :]
        for i, w in enumerate(weights)
    ]
    return parts[0] if len(parts) == 1 else jnp.where(at < count, parts[0], parts[1])


def products(blocks, ids, at, weights):
    total = None
    for b, block in enumerate(blocks):
        rows = [ids[LINES * (at + b) + k] for k in range(LINES)]
        met = jnp.concatenate(
            [jnp.concatenate([met_rows(weights, s, r) for s in range(3)], axis=1) for r in rows], axis=0
        )
        part = jnp.dot(block[...], met, preferred_element_type=jnp.float32)
        total = part if total is None else total + part
    return [total[:, s * LANES : (s + 1) * LANES] for s in range(3)]


def project_kernel(count, kinds, at, ids, *refs):
    weights, refs = refs[:kinds], refs[kinds:]
    blocks, sums, out = refs[:count], refs[count:-1], refs[-1]
    for s, part in enumerate(products(blocks, ids, at, weights)):
        out[s] = sums[0][s] + part if sums else part


def project(sums, blocks, ids, at, in_weights):
    extra = [] if sums is None else [sums]
    rows = blocks[0].shape[0]
    return pl.pallas_call(
        functools.partial(project_kernel, len(blocks), len(in_weights), at),
        in_specs=[SMEM] + [VMEM] * (len(in_weights) + len(blocks) + len(extra)),
        out_specs=VMEM,
        out_shape=jax.ShapeDtypeStruct((3, rows, LANES), jnp.float32),
        input_output_aliases={1 + len(in_weights) + len(blocks): 0} if extra else {},
        compiler_params=pltpu.CompilerParams(vmem_limit_bytes=16 * 2**20),
        cost_estimate=pl.CostEstimate(flops=rows, bytes_accessed=rows, transcendentals=0),
    )(ids, *in_weights, *blocks, *extra)


def local_kernel(count, kinds, summed, at, seat, ids, taps, weights, decays, skip, *refs):
    sums, refs = refs[:summed], refs[summed:]
    in_weights, blocks, (pack, sent, proj, ends) = refs[:kinds], refs[kinds : kinds + count], refs[-4:]
    rows = blocks[0].shape[0] - HALO
    length = rows // CHUNKS
    early = TAPS - 1
    top = lax.broadcasted_iota(jnp.int32, (CHUNKS, LANES), 0) == 0
    for s, part in enumerate(products(blocks, ids, at, in_weights)):
        total = sums[0][s] + part if sums else part
        proj[s, early * CHUNKS :, :] = total[HALO:]
        for p in range(early):
            end = pltpu.roll(proj[s, (length + p) * CHUNKS : (length + p + 1) * CHUNKS, :], 1, 0)
            proj[s, p * CHUNKS : (p + 1) * CHUNKS, :] = jnp.where(
                top, wide(total[HALO - early + p : HALO - early + p + 1]), end
            )
    poles = [wide(jnp.exp(-decays[m : m + 1, :])) for m in range(MODES)]
    gains = [wide(weights[m : m + 1, :]) for m in range(MODES)]
    skip_row = wide(skip[0:1, :])

    def steps(at, states):
        states = list(states)
        at = at * UNROLL
        taken = [
            [
                proj[s, pl.ds(pl.multiple_of((at + k) * CHUNKS, CHUNKS), CHUNKS), :]
                for k in range(UNROLL + TAPS - 1)
            ]
            for s in range(3)
        ]
        coef = [[wide(taps[s, j : j + 1, :]) for j in range(TAPS)] for s in range(3)]
        for u in range(UNROLL):
            filtered = [sum(coef[s][j] * taken[s][u + j] for j in range(TAPS)) for s in range(3)]
            gated = filtered[1] * filtered[2]
            total = skip_row * gated
            for m in range(MODES):
                states[m] = poles[m] * states[m] + gated
                total = total + gains[m] * states[m]
            here = pl.multiple_of((at + u) * CHUNKS, CHUNKS)
            pack[pl.ds(here, CHUNKS), :] = filtered[0]
            pack[pl.ds(rows + here, CHUNKS), :] = filtered[0] * total
        return tuple(states)

    zero = jnp.zeros((CHUNKS, LANES), jnp.float32)
    states = lax.fori_loop(0, length // UNROLL, steps, (zero,) * MODES)
    for m in range(MODES):
        ends[m * CHUNKS : (m + 1) * CHUNKS, :] = states[m]
    over = jnp.exp(-decays[...] * float(length))
    carry = jnp.zeros((MODES, LANES), jnp.float32)
    for c in range(CHUNKS):
        pack[2 * rows + c * MODES : 2 * rows + (c + 1) * MODES, :] = carry
        carry = over * carry + ends[pl.ds(c, MODES, stride=CHUNKS), :]
    pack[2 * rows + CHUNKS * MODES : 2 * rows + (CHUNKS + 1) * MODES, :] = carry
    mine, half, owner = seat[0], seat[1], seat[2]
    for j in range(sent.shape[1]):
        ahead = j - mine - 1
        distance = (jnp.maximum(ahead, 0) * 2 * rows + (1 - half) * rows).astype(jnp.float32)
        sent[owner, j] = jnp.where(ahead >= 0, jnp.exp(-decays[...] * distance) * carry, 0.0)


def local_part(sent, sums, blocks, seat, ids, at, in_weights, taps, weights, decays, skip, count):
    rows = blocks[0].shape[0] - HALO
    extra = [] if sent is None else [sent]
    summed = [] if sums is None else [sums]
    return pl.pallas_call(
        functools.partial(local_kernel, len(blocks), len(in_weights), len(summed), at),
        in_specs=[SMEM] * 2 + [VMEM] * (4 + len(summed) + len(in_weights) + len(blocks) + len(extra)),
        out_specs=[VMEM] * 2,
        out_shape=[
            jax.ShapeDtypeStruct((2 * rows + (CHUNKS + 1) * MODES, LANES), jnp.float32),
            jax.ShapeDtypeStruct((2, count, MODES, LANES), jnp.float32),
        ],
        input_output_aliases={6 + len(summed) + len(in_weights) + len(blocks): 1} if extra else {},
        scratch_shapes=[
            pltpu.VMEM((3, rows + (TAPS - 1) * CHUNKS, LANES), jnp.float32),
            pltpu.VMEM((MODES * CHUNKS, LANES), jnp.float32),
        ],
        compiler_params=pltpu.CompilerParams(vmem_limit_bytes=16 * 2**20),
        cost_estimate=pl.CostEstimate(
            flops=rows * LANES * 110, bytes_accessed=rows * LANES * 20, transcendentals=0
        ),
    )(seat, ids, taps, weights, decays, skip, *summed, *in_weights, *blocks, *extra)


def final_kernel(rows, seat, arrived, mine, other, weights, decays, out, begins):
    length = rows // CHUNKS
    half = seat[1]
    low = half == 0
    end = slice(2 * rows + CHUNKS * MODES, 2 * rows + (CHUNKS + 1) * MODES)
    poles = [wide(jnp.exp(-decays[m : m + 1, :])) for m in range(MODES)]
    over = jnp.exp(-decays[...] * float(length))
    beyond = jnp.exp(-decays[...] * float(rows))
    early = sum(arrived[k] for k in range(arrived.shape[0]))
    late = beyond * early + jnp.where(low, mine[end, :], other[end, :])
    for pack, begin, offset in (
        (mine, jnp.where(low, early, late), half * rows),
        (other, jnp.where(low, late, early), (1 - half) * rows),
    ):
        reach = jnp.ones_like(over)
        for c in range(CHUNKS):
            start = pack[2 * rows + c * MODES : 2 * rows + (c + 1) * MODES, :]
            begins[pl.ds(c, MODES, stride=CHUNKS), :] = weights[...] * (start + reach * begin)
            reach = reach * over

        def steps(at, terms, pack=pack, offset=offset):
            terms = list(terms)
            at = at * UNROLL
            for u in range(UNROLL):
                terms = [poles[m] * terms[m] for m in range(MODES)]
                sums = terms
                while len(sums) > 1:
                    sums = [sums[i] + sums[i + 1] for i in range(0, len(sums), 2)]
                here = pl.multiple_of((at + u) * CHUNKS, CHUNKS)
                out[pl.ds(offset + at + u, CHUNKS, stride=length), :] = (
                    pack[pl.ds(rows + here, CHUNKS), :] + pack[pl.ds(here, CHUNKS), :] * sums[0]
                )
            return tuple(terms)

        terms = tuple(begins[m * CHUNKS : (m + 1) * CHUNKS, :] for m in range(MODES))
        lax.fori_loop(0, length // UNROLL, steps, terms)


def final_part(seat, arrived, mine, other, weights, decays):
    rows = (mine.shape[0] - (CHUNKS + 1) * MODES) // 2
    return pl.pallas_call(
        functools.partial(final_kernel, rows),
        in_specs=[SMEM] + [VMEM] * 5,
        out_specs=VMEM,
        out_shape=jax.ShapeDtypeStruct((2 * rows, LANES), jnp.float32),
        scratch_shapes=[pltpu.VMEM((MODES * CHUNKS, LANES), jnp.float32)],
        compiler_params=pltpu.CompilerParams(vmem_limit_bytes=16 * 2**20),
        cost_estimate=pl.CostEstimate(
            flops=rows * LANES * 72, bytes_accessed=rows * LANES * 24, transcendentals=0
        ),
    )(seat, arrived, mine, other, weights, decays)


def per_device(tokens, in_weights, short_taps, residues, decays, skip_gain):
    rows = tokens.shape[0]
    part = rows // 2
    blocks = lax.axis_size("ctx")
    ring, lines = RING, LINES
    mine = lax.axis_index("ctx")
    place = mine * lines * ring + lax.axis_index("ch")
    half = lax.axis_index("ch") // ring % 2
    weights = (residues * jnp.sqrt(2.0 * decays / MODES)).T
    rates = decays.T

    def beside(block, step):
        return lax.ppermute(
            block, "ch", [(z * ring + y, (z ^ step) * ring + y) for z in range(lines) for y in range(ring)]
        )

    def onward(block):
        route = []
        for i in range(blocks):
            for z in range(lines):
                for y in range(ring):
                    at = (i * lines + z) * ring
                    route.append((at + y, at + (y + 1 - i % 2 * 2) % ring))
        return lax.ppermute(block, ("ctx", "ch"), route)

    def other_core(block):
        return lax.ppermute(block, "ctx", [(i, i ^ 1) for i in range(blocks)])

    table = np.zeros((2, 2, lines, ring, ring, lines), np.int32)
    for c, z, y, k in np.ndindex(2, lines, ring, lines):
        way = 1 - 2 * c
        places = [y] + [y + way * d for step in range(1, ring // 2) for d in (-step, step)] + [y + ring // 2]
        ids = (z ^ k) * ring + np.array(places) % ring
        count = lines * ring // 2
        table[c, 0, z, y, :, k] = ids
        table[c, 1, z, y, :, k] = ids % count + count * (ids // count != c)
    table = table.transpose(0, 2, 3, 1, 4, 5).reshape(2, lines * ring, -1)[np.arange(blocks) % 2]
    ids = lax.dynamic_index_in_dim(
        jnp.asarray(table.reshape(-1, 2 * lines * ring)), place, 0, keepdims=False
    )

    seat = jnp.stack([mine, half, half]).astype(jnp.int32)
    other_seat = jnp.stack([mine, half, 1 - half]).astype(jnp.int32)

    before = lax.ppermute(tokens[rows - HALO :], "ctx", [(i, i + 1) for i in range(blocks - 1)])
    ordered = tokens.reshape(2, CHUNKS, part // CHUNKS, -1).swapaxes(1, 2).reshape(2, part, -1)
    between = tokens[part - HALO : part]
    low = half == 0
    kept = jnp.concatenate([jnp.where(low, before, between), jnp.where(low, ordered[0], ordered[1])], axis=0)
    given = jnp.concatenate([jnp.where(low, between, before), jnp.where(low, ordered[1], ordered[0])], axis=0)
    nearest = beside(given, 1)
    count = in_weights.shape[1] // 2
    sliced = lax.dynamic_slice_in_dim(in_weights, mine % 2 * count, count, 1)
    values = jnp.concatenate([short_taps.reshape(3 * TAPS, -1), weights, rates, skip_gain[None, :]], axis=0)
    half_weights, values = beside(after(sliced, nearest), 1), beside(values, 1)
    block = jnp.concatenate([kept, nearest, beside(kept, 2), beside(given, 3)], axis=1)

    block = after(after(block, values), sliced)
    straight, turned = onward(block), other_core(block)
    crossed = onward(turned)
    sums, waiting, met = None, [block], 0
    arrived = []
    for step in range(1, ring // 2):
        straight, turned = lax.optimization_barrier((straight, turned))
        crossed, here = lax.optimization_barrier((crossed, straight))
        turned = crossed
        if step == ring // 2 - 1:
            crossed = after(after(crossed, waiting[1]), half_weights)
        straight = onward(straight)
        swapped = other_core(crossed)
        if step < ring // 2 - 1:
            crossed = onward(crossed)
        sums = project(sums, waiting, ids, met, [in_weights])
        arrived += waiting
        met += len(waiting)
        waiting = [here, swapped]
        if step < ring // 2 - 1:
            straight, sums = lax.optimization_barrier((straight, sums))
    half_weights = after(after(half_weights, straight), swapped)
    their_weights = [half_weights, other_core(half_weights)]
    waiting.append(straight)
    pack, sent = local_part(
        None, sums, waiting, seat, ids, met, [in_weights], short_taps, weights, rates, skip_gain[None, :], blocks
    )
    other_pack, sent = local_part(
        sent, None, arrived + waiting, other_seat, ids, ring, their_weights,
        values[: 3 * TAPS].reshape(3, TAPS, -1),
        values[3 * TAPS : 3 * TAPS + MODES],
        values[3 * TAPS + MODES : 3 * TAPS + 2 * MODES],
        values[3 * TAPS + 2 * MODES :],
        blocks,
    )
    other = beside(other_pack, 1)
    groups = [
        [(i * lines + z + q) * ring + y for q in range(2) for i in range(blocks)]
        for z in range(0, lines, 2)
        for y in range(ring)
    ]
    states = lax.all_to_all(
        sent.reshape(2 * blocks, MODES, LANES), ("ctx", "ch"), 0, 0, axis_index_groups=groups, tiled=True
    )
    return final_part(seat, states, pack, other, weights, rates)


def solution(mesh):
    return jax.shard_map(
        per_device,
        mesh=mesh,
        in_specs=(
            P("ctx", "ch"),
            P(None, None, "ch"),
            P(None, None, "ch"),
            P("ch", None),
            P("ch", None),
            P("ch"),
        ),
        out_specs=P("ctx", "ch"),
        check_vma=False,
    )
```

```python
import functools

import jax
import jax.numpy as jnp
import numpy as np
from jax import lax
from jax.experimental import pallas as pl
from jax.experimental.pallas import tpu as pltpu
from jax.sharding import PartitionSpec as P

MODES = 16
TAPS = 7
HALO = 16
CHUNKS = 8
UNROLL = 8
LANES = 128
RING = 8
LINES = 4
SMEM = pl.BlockSpec(memory_space=pltpu.SMEM)
VMEM = pl.BlockSpec(memory_space=pltpu.VMEM)


def after(value, earlier):
    return lax.optimization_barrier((value, earlier))[0]


def wide(row):
    return jnp.broadcast_to(row, (CHUNKS, LANES))


def met_rows(weights, s, at):
    count = weights[0].shape[1] // LANES
    parts = [
        w[s, pl.ds(pl.multiple_of(jnp.clip(at - i * count, 0, count - 1) * LANES, LANES), LANES), :]
        for i, w in enumerate(weights)
    ]
    return parts[0] if len(parts) == 1 else jnp.where(at < count, parts[0], parts[1])


def products(blocks, ids, at, weights):
    total = None
    for b, block in enumerate(blocks):
        rows = [ids[LINES * (at + b) + k] for k in range(LINES)]
        met = jnp.concatenate(
            [jnp.concatenate([met_rows(weights, s, r) for s in range(3)], axis=1) for r in rows], axis=0
        )
        part = jnp.dot(block[...], met, preferred_element_type=jnp.float32)
        total = part if total is None else total + part
    return [total[:, s * LANES : (s + 1) * LANES] for s in range(3)]


def project_kernel(count, kinds, at, ids, *refs):
    weights, refs = refs[:kinds], refs[kinds:]
    blocks, sums, out = refs[:count], refs[count:-1], refs[-1]
    for s, part in enumerate(products(blocks, ids, at, weights)):
        out[s] = sums[0][s] + part if sums else part


def project(sums, blocks, ids, at, in_weights):
    extra = [] if sums is None else [sums]
    rows = blocks[0].shape[0]
    return pl.pallas_call(
        functools.partial(project_kernel, len(blocks), len(in_weights), at),
        in_specs=[SMEM] + [VMEM] * (len(in_weights) + len(blocks) + len(extra)),
        out_specs=VMEM,
        out_shape=jax.ShapeDtypeStruct((3, rows, LANES), jnp.float32),
        input_output_aliases={1 + len(in_weights) + len(blocks): 0} if extra else {},
        compiler_params=pltpu.CompilerParams(vmem_limit_bytes=16 * 2**20),
        cost_estimate=pl.CostEstimate(flops=rows, bytes_accessed=rows, transcendentals=0),
    )(ids, *in_weights, *blocks, *extra)


def local_kernel(count, kinds, summed, at, seat, ids, taps, weights, decays, skip, *refs):
    sums, refs = refs[:summed], refs[summed:]
    in_weights, blocks, (pack, sent, proj, ends) = refs[:kinds], refs[kinds : kinds + count], refs[-4:]
    rows = blocks[0].shape[0] - HALO
    length = rows // CHUNKS
    early = TAPS - 1
    top = lax.broadcasted_iota(jnp.int32, (CHUNKS, LANES), 0) == 0
    for s, part in enumerate(products(blocks, ids, at, in_weights)):
        total = sums[0][s] + part if sums else part
        proj[s, early * CHUNKS :, :] = total[HALO:]
        for p in range(early):
            end = pltpu.roll(proj[s, (length + p) * CHUNKS : (length + p + 1) * CHUNKS, :], 1, 0)
            proj[s, p * CHUNKS : (p + 1) * CHUNKS, :] = jnp.where(
                top, wide(total[HALO - early + p : HALO - early + p + 1]), end
            )
    poles = [wide(jnp.exp(-decays[m : m + 1, :])) for m in range(MODES)]
    gains = [wide(weights[m : m + 1, :]) for m in range(MODES)]
    skip_row = wide(skip[0:1, :])

    def steps(at, states):
        states = list(states)
        at = at * UNROLL
        taken = [
            [
                proj[s, pl.ds(pl.multiple_of((at + k) * CHUNKS, CHUNKS), CHUNKS), :]
                for k in range(UNROLL + TAPS - 1)
            ]
            for s in range(3)
        ]
        coef = [[wide(taps[s, j : j + 1, :]) for j in range(TAPS)] for s in range(3)]
        for u in range(UNROLL):
            filtered = [sum(coef[s][j] * taken[s][u + j] for j in range(TAPS)) for s in range(3)]
            gated = filtered[1] * filtered[2]
            total = skip_row * gated
            for m in range(MODES):
                states[m] = poles[m] * states[m] + gated
                total = total + gains[m] * states[m]
            here = pl.multiple_of((at + u) * CHUNKS, CHUNKS)
            pack[pl.ds(here, CHUNKS), :] = filtered[0]
            pack[pl.ds(rows + here, CHUNKS), :] = filtered[0] * total
        return tuple(states)

    zero = jnp.zeros((CHUNKS, LANES), jnp.float32)
    states = lax.fori_loop(0, length // UNROLL, steps, (zero,) * MODES)
    for m in range(MODES):
        ends[m * CHUNKS : (m + 1) * CHUNKS, :] = states[m]
    over = jnp.exp(-decays[...] * float(length))
    carry = jnp.zeros((MODES, LANES), jnp.float32)
    for c in range(CHUNKS):
        pack[2 * rows + c * MODES : 2 * rows + (c + 1) * MODES, :] = carry
        carry = over * carry + ends[pl.ds(c, MODES, stride=CHUNKS), :]
    pack[2 * rows + CHUNKS * MODES : 2 * rows + (CHUNKS + 1) * MODES, :] = carry
    mine, half, owner = seat[0], seat[1], seat[2]
    for j in range(sent.shape[1]):
        ahead = j - mine - 1
        distance = (jnp.maximum(ahead, 0) * 2 * rows + (1 - half) * rows).astype(jnp.float32)
        sent[owner, j] = jnp.where(ahead >= 0, jnp.exp(-decays[...] * distance) * carry, 0.0)


def local_part(sent, sums, blocks, seat, ids, at, in_weights, taps, weights, decays, skip, count):
    rows = blocks[0].shape[0] - HALO
    extra = [] if sent is None else [sent]
    summed = [] if sums is None else [sums]
    return pl.pallas_call(
        functools.partial(local_kernel, len(blocks), len(in_weights), len(summed), at),
        in_specs=[SMEM] * 2 + [VMEM] * (4 + len(summed) + len(in_weights) + len(blocks) + len(extra)),
        out_specs=[VMEM] * 2,
        out_shape=[
            jax.ShapeDtypeStruct((2 * rows + (CHUNKS + 1) * MODES, LANES), jnp.float32),
            jax.ShapeDtypeStruct((2, count, MODES, LANES), jnp.float32),
        ],
        input_output_aliases={6 + len(summed) + len(in_weights) + len(blocks): 1} if extra else {},
        scratch_shapes=[
            pltpu.VMEM((3, rows + (TAPS - 1) * CHUNKS, LANES), jnp.float32),
            pltpu.VMEM((MODES * CHUNKS, LANES), jnp.float32),
        ],
        compiler_params=pltpu.CompilerParams(vmem_limit_bytes=16 * 2**20),
        cost_estimate=pl.CostEstimate(
            flops=rows * LANES * 110, bytes_accessed=rows * LANES * 20, transcendentals=0
        ),
    )(seat, ids, taps, weights, decays, skip, *summed, *in_weights, *blocks, *extra)


def final_kernel(rows, seat, arrived, mine, other, weights, decays, out, begins):
    length = rows // CHUNKS
    half = seat[1]
    low = half == 0
    end = slice(2 * rows + CHUNKS * MODES, 2 * rows + (CHUNKS + 1) * MODES)
    poles = [wide(jnp.exp(-decays[m : m + 1, :])) for m in range(MODES)]
    over = jnp.exp(-decays[...] * float(length))
    beyond = jnp.exp(-decays[...] * float(rows))
    early = sum(arrived[k] for k in range(arrived.shape[0]))
    late = beyond * early + jnp.where(low, mine[end, :], other[end, :])
    for pack, begin, offset in (
        (mine, jnp.where(low, early, late), half * rows),
        (other, jnp.where(low, late, early), (1 - half) * rows),
    ):
        reach = jnp.ones_like(over)
        for c in range(CHUNKS):
            start = pack[2 * rows + c * MODES : 2 * rows + (c + 1) * MODES, :]
            begins[pl.ds(c, MODES, stride=CHUNKS), :] = weights[...] * (start + reach * begin)
            reach = reach * over

        def steps(at, terms, pack=pack, offset=offset):
            terms = list(terms)
            at = at * UNROLL
            for u in range(UNROLL):
                terms = [poles[m] * terms[m] for m in range(MODES)]
                sums = terms
                while len(sums) > 1:
                    sums = [sums[i] + sums[i + 1] for i in range(0, len(sums), 2)]
                here = pl.multiple_of((at + u) * CHUNKS, CHUNKS)
                out[pl.ds(offset + at + u, CHUNKS, stride=length), :] = (
                    pack[pl.ds(rows + here, CHUNKS), :] + pack[pl.ds(here, CHUNKS), :] * sums[0]
                )
            return tuple(terms)

        terms = tuple(begins[m * CHUNKS : (m + 1) * CHUNKS, :] for m in range(MODES))
        lax.fori_loop(0, length // UNROLL, steps, terms)


def final_part(seat, arrived, mine, other, weights, decays):
    rows = (mine.shape[0] - (CHUNKS + 1) * MODES) // 2
    return pl.pallas_call(
        functools.partial(final_kernel, rows),
        in_specs=[SMEM] + [VMEM] * 5,
        out_specs=VMEM,
        out_shape=jax.ShapeDtypeStruct((2 * rows, LANES), jnp.float32),
        scratch_shapes=[pltpu.VMEM((MODES * CHUNKS, LANES), jnp.float32)],
        compiler_params=pltpu.CompilerParams(vmem_limit_bytes=16 * 2**20),
        cost_estimate=pl.CostEstimate(
            flops=rows * LANES * 72, bytes_accessed=rows * LANES * 24, transcendentals=0
        ),
    )(seat, arrived, mine, other, weights, decays)


def per_device(tokens, in_weights, short_taps, residues, decays, skip_gain):
    rows = tokens.shape[0]
    part = rows // 2
    blocks = lax.axis_size("ctx")
    ring, lines = RING, LINES
    mine = lax.axis_index("ctx")
    place = mine * lines * ring + lax.axis_index("ch")
    half = lax.axis_index("ch") // ring % 2
    weights = (residues * jnp.sqrt(2.0 * decays / MODES)).T
    rates = decays.T

    def beside(block, step):
        return lax.ppermute(
            block, "ch", [(z * ring + y, (z ^ step) * ring + y) for z in range(lines) for y in range(ring)]
        )

    def onward(block):
        route = []
        for i in range(blocks):
            for z in range(lines):
                for y in range(ring):
                    at = (i * lines + z) * ring
                    route.append((at + y, at + (y + 1 - i % 2 * 2) % ring))
        return lax.ppermute(block, ("ctx", "ch"), route)

    def other_core(block):
        return lax.ppermute(block, "ctx", [(i, i ^ 1) for i in range(blocks)])

    table = np.zeros((2, 2, lines, ring, ring, lines), np.int32)
    for c, z, y, k in np.ndindex(2, lines, ring, lines):
        way = 1 - 2 * c
        places = [y] + [y + way * d for step in range(1, ring // 2) for d in (-step, step)] + [y + ring // 2]
        ids = (z ^ k) * ring + np.array(places) % ring
        count = lines * ring // 2
        table[c, 0, z, y, :, k] = ids
        table[c, 1, z, y, :, k] = ids % count + count * (ids // count != c)
    table = table.transpose(0, 2, 3, 1, 4, 5).reshape(2, lines * ring, -1)[np.arange(blocks) % 2]
    ids = lax.dynamic_index_in_dim(
        jnp.asarray(table.reshape(-1, 2 * lines * ring)), place, 0, keepdims=False
    )

    seat = jnp.stack([mine, half, half]).astype(jnp.int32)
    other_seat = jnp.stack([mine, half, 1 - half]).astype(jnp.int32)

    before = lax.ppermute(tokens[rows - HALO :], "ctx", [(i, i + 1) for i in range(blocks - 1)])
    ordered = tokens.reshape(2, CHUNKS, part // CHUNKS, -1).swapaxes(1, 2).reshape(2, part, -1)
    between = tokens[part - HALO : part]
    low = half == 0
    kept = jnp.concatenate([jnp.where(low, before, between), jnp.where(low, ordered[0], ordered[1])], axis=0)
    given = jnp.concatenate([jnp.where(low, between, before), jnp.where(low, ordered[1], ordered[0])], axis=0)
    nearest = beside(given, 1)
    count = in_weights.shape[1] // 2
    sliced = lax.dynamic_slice_in_dim(in_weights, mine % 2 * count, count, 1)
    values = jnp.concatenate([short_taps.reshape(3 * TAPS, -1), weights, rates, skip_gain[None, :]], axis=0)
    values = after(values, before)
    half_weights, values = beside(after(sliced, nearest), 1), beside(values, 1)
    block = jnp.concatenate([kept, nearest, beside(kept, 2), beside(given, 3)], axis=1)

    block = after(after(block, values), sliced)
    straight, turned = onward(block), other_core(block)
    crossed = onward(turned)
    sums, waiting, met = None, [block], 0
    arrived = []
    for step in range(1, ring // 2):
        straight, turned = lax.optimization_barrier((straight, turned))
        crossed, here = lax.optimization_barrier((crossed, straight))
        turned = crossed
        if step == ring // 2 - 1:
            crossed = after(after(crossed, waiting[1]), half_weights)
        straight = onward(straight)
        swapped = other_core(crossed)
        if step < ring // 2 - 1:
            crossed = onward(crossed)
        sums = project(sums, waiting, ids, met, [in_weights])
        arrived += waiting
        met += len(waiting)
        waiting = [here, swapped]
        if step < ring // 2 - 1:
            straight, sums = lax.optimization_barrier((straight, sums))
    half_weights = after(after(half_weights, straight), swapped)
    their_weights = [half_weights, other_core(half_weights)]
    waiting.append(straight)
    pack, sent = local_part(
        None, sums, waiting, seat, ids, met, [in_weights], short_taps, weights, rates, skip_gain[None, :], blocks
    )
    other_pack, sent = local_part(
        sent, None, arrived + waiting, other_seat, ids, ring, their_weights,
        values[: 3 * TAPS].reshape(3, TAPS, -1),
        values[3 * TAPS : 3 * TAPS + MODES],
        values[3 * TAPS + MODES : 3 * TAPS + 2 * MODES],
        values[3 * TAPS + 2 * MODES :],
        blocks,
    )
    other = beside(other_pack, 1)
    groups = [
        [(i * lines + z + q) * ring + y for q in range(2) for i in range(blocks)]
        for z in range(0, lines, 2)
        for y in range(ring)
    ]
    states = lax.all_to_all(
        sent.reshape(2 * blocks, MODES, LANES), ("ctx", "ch"), 0, 0, axis_index_groups=groups, tiled=True
    )
    return final_part(seat, states, pack, other, weights, rates)


def solution(mesh):
    return jax.shard_map(
        per_device,
        mesh=mesh,
        in_specs=(
            P("ctx", "ch"),
            P(None, None, "ch"),
            P(None, None, "ch"),
            P("ch", None),
            P("ch", None),
            P("ch"),
        ),
        out_specs=P("ctx", "ch"),
        check_vma=False,
    )
```

```python
import functools

import jax
import jax.numpy as jnp
import numpy as np
from jax import lax
from jax.experimental import pallas as pl
from jax.experimental.pallas import tpu as pltpu
from jax.sharding import PartitionSpec as P

MODES = 16
TAPS = 7
HALO = 16
CHUNKS = 8
UNROLL = 16
LANES = 128
RING = 8
LINES = 4
SMEM = pl.BlockSpec(memory_space=pltpu.SMEM)
VMEM = pl.BlockSpec(memory_space=pltpu.VMEM)


def after(value, earlier):
    return lax.optimization_barrier((value, earlier))[0]


def wide(row):
    return jnp.broadcast_to(row, (CHUNKS, LANES))


def met_rows(weights, s, at):
    count = weights[0].shape[1] // LANES
    parts = [
        w[s, pl.ds(pl.multiple_of(jnp.clip(at - i * count, 0, count - 1) * LANES, LANES), LANES), :]
        for i, w in enumerate(weights)
    ]
    return parts[0] if len(parts) == 1 else jnp.where(at < count, parts[0], parts[1])


def products(blocks, ids, at, weights):
    total = None
    for b, block in enumerate(blocks):
        rows = [ids[LINES * (at + b) + k] for k in range(LINES)]
        met = jnp.concatenate(
            [jnp.concatenate([met_rows(weights, s, r) for s in range(3)], axis=1) for r in rows], axis=0
        )
        part = jnp.dot(block[...], met, preferred_element_type=jnp.float32)
        total = part if total is None else total + part
    return [total[:, s * LANES : (s + 1) * LANES] for s in range(3)]


def project_kernel(count, kinds, at, ids, *refs):
    weights, refs = refs[:kinds], refs[kinds:]
    blocks, sums, out = refs[:count], refs[count:-1], refs[-1]
    for s, part in enumerate(products(blocks, ids, at, weights)):
        out[s] = sums[0][s] + part if sums else part


def project(sums, blocks, ids, at, in_weights):
    extra = [] if sums is None else [sums]
    rows = blocks[0].shape[0]
    return pl.pallas_call(
        functools.partial(project_kernel, len(blocks), len(in_weights), at),
        in_specs=[SMEM] + [VMEM] * (len(in_weights) + len(blocks) + len(extra)),
        out_specs=VMEM,
        out_shape=jax.ShapeDtypeStruct((3, rows, LANES), jnp.float32),
        input_output_aliases={1 + len(in_weights) + len(blocks): 0} if extra else {},
        compiler_params=pltpu.CompilerParams(vmem_limit_bytes=16 * 2**20),
        cost_estimate=pl.CostEstimate(flops=rows, bytes_accessed=rows, transcendentals=0),
    )(ids, *in_weights, *blocks, *extra)


def local_kernel(count, kinds, summed, at, seat, ids, taps, weights, decays, skip, *refs):
    sums, refs = refs[:summed], refs[summed:]
    in_weights, blocks, (pack, sent, proj, ends) = refs[:kinds], refs[kinds : kinds + count], refs[-4:]
    rows = blocks[0].shape[0] - HALO
    length = rows // CHUNKS
    early = TAPS - 1
    top = lax.broadcasted_iota(jnp.int32, (CHUNKS, LANES), 0) == 0
    for s, part in enumerate(products(blocks, ids, at, in_weights)):
        total = sums[0][s] + part if sums else part
        proj[s, early * CHUNKS :, :] = total[HALO:]
        for p in range(early):
            end = pltpu.roll(proj[s, (length + p) * CHUNKS : (length + p + 1) * CHUNKS, :], 1, 0)
            proj[s, p * CHUNKS : (p + 1) * CHUNKS, :] = jnp.where(
                top, wide(total[HALO - early + p : HALO - early + p + 1]), end
            )
    poles = [wide(jnp.exp(-decays[m : m + 1, :])) for m in range(MODES)]
    gains = [wide(weights[m : m + 1, :]) for m in range(MODES)]
    skip_row = wide(skip[0:1, :])

    def steps(at, states):
        states = list(states)
        at = at * UNROLL
        taken = [
            [
                proj[s, pl.ds(pl.multiple_of((at + k) * CHUNKS, CHUNKS), CHUNKS), :]
                for k in range(UNROLL + TAPS - 1)
            ]
            for s in range(3)
        ]
        coef = [[wide(taps[s, j : j + 1, :]) for j in range(TAPS)] for s in range(3)]
        for u in range(UNROLL):
            filtered = [sum(coef[s][j] * taken[s][u + j] for j in range(TAPS)) for s in range(3)]
            gated = filtered[1] * filtered[2]
            total = skip_row * gated
            for m in range(MODES):
                states[m] = poles[m] * states[m] + gated
                total = total + gains[m] * states[m]
            here = pl.multiple_of((at + u) * CHUNKS, CHUNKS)
            pack[pl.ds(here, CHUNKS), :] = filtered[0]
            pack[pl.ds(rows + here, CHUNKS), :] = filtered[0] * total
        return tuple(states)

    zero = jnp.zeros((CHUNKS, LANES), jnp.float32)
    states = lax.fori_loop(0, length // UNROLL, steps, (zero,) * MODES)
    for m in range(MODES):
        ends[m * CHUNKS : (m + 1) * CHUNKS, :] = states[m]
    over = jnp.exp(-decays[...] * float(length))
    carry = jnp.zeros((MODES, LANES), jnp.float32)
    for c in range(CHUNKS):
        pack[2 * rows + c * MODES : 2 * rows + (c + 1) * MODES, :] = carry
        carry = over * carry + ends[pl.ds(c, MODES, stride=CHUNKS), :]
    pack[2 * rows + CHUNKS * MODES : 2 * rows + (CHUNKS + 1) * MODES, :] = carry
    mine, half, owner = seat[0], seat[1], seat[2]
    for j in range(sent.shape[1]):
        ahead = j - mine - 1
        distance = (jnp.maximum(ahead, 0) * 2 * rows + (1 - half) * rows).astype(jnp.float32)
        sent[owner, j] = jnp.where(ahead >= 0, jnp.exp(-decays[...] * distance) * carry, 0.0)


def local_part(sent, sums, blocks, seat, ids, at, in_weights, taps, weights, decays, skip, count):
    rows = blocks[0].shape[0] - HALO
    extra = [] if sent is None else [sent]
    summed = [] if sums is None else [sums]
    return pl.pallas_call(
        functools.partial(local_kernel, len(blocks), len(in_weights), len(summed), at),
        in_specs=[SMEM] * 2 + [VMEM] * (4 + len(summed) + len(in_weights) + len(blocks) + len(extra)),
        out_specs=[VMEM] * 2,
        out_shape=[
            jax.ShapeDtypeStruct((2 * rows + (CHUNKS + 1) * MODES, LANES), jnp.float32),
            jax.ShapeDtypeStruct((2, count, MODES, LANES), jnp.float32),
        ],
        input_output_aliases={6 + len(summed) + len(in_weights) + len(blocks): 1} if extra else {},
        scratch_shapes=[
            pltpu.VMEM((3, rows + (TAPS - 1) * CHUNKS, LANES), jnp.float32),
            pltpu.VMEM((MODES * CHUNKS, LANES), jnp.float32),
        ],
        compiler_params=pltpu.CompilerParams(vmem_limit_bytes=16 * 2**20),
        cost_estimate=pl.CostEstimate(
            flops=rows * LANES * 110, bytes_accessed=rows * LANES * 20, transcendentals=0
        ),
    )(seat, ids, taps, weights, decays, skip, *summed, *in_weights, *blocks, *extra)


def final_kernel(rows, seat, arrived, mine, other, weights, decays, out, begins):
    length = rows // CHUNKS
    half = seat[1]
    low = half == 0
    end = slice(2 * rows + CHUNKS * MODES, 2 * rows + (CHUNKS + 1) * MODES)
    poles = [wide(jnp.exp(-decays[m : m + 1, :])) for m in range(MODES)]
    over = jnp.exp(-decays[...] * float(length))
    beyond = jnp.exp(-decays[...] * float(rows))
    early = sum(arrived[k] for k in range(arrived.shape[0]))
    late = beyond * early + jnp.where(low, mine[end, :], other[end, :])
    for pack, begin, offset in (
        (mine, jnp.where(low, early, late), half * rows),
        (other, jnp.where(low, late, early), (1 - half) * rows),
    ):
        reach = jnp.ones_like(over)
        for c in range(CHUNKS):
            start = pack[2 * rows + c * MODES : 2 * rows + (c + 1) * MODES, :]
            begins[pl.ds(c, MODES, stride=CHUNKS), :] = weights[...] * (start + reach * begin)
            reach = reach * over

        def steps(at, terms, pack=pack, offset=offset):
            terms = list(terms)
            at = at * UNROLL
            for u in range(UNROLL):
                terms = [poles[m] * terms[m] for m in range(MODES)]
                sums = terms
                while len(sums) > 1:
                    sums = [sums[i] + sums[i + 1] for i in range(0, len(sums), 2)]
                here = pl.multiple_of((at + u) * CHUNKS, CHUNKS)
                out[pl.ds(offset + at + u, CHUNKS, stride=length), :] = (
                    pack[pl.ds(rows + here, CHUNKS), :] + pack[pl.ds(here, CHUNKS), :] * sums[0]
                )
            return tuple(terms)

        terms = tuple(begins[m * CHUNKS : (m + 1) * CHUNKS, :] for m in range(MODES))
        lax.fori_loop(0, length // UNROLL, steps, terms)


def final_part(seat, arrived, mine, other, weights, decays):
    rows = (mine.shape[0] - (CHUNKS + 1) * MODES) // 2
    return pl.pallas_call(
        functools.partial(final_kernel, rows),
        in_specs=[SMEM] + [VMEM] * 5,
        out_specs=VMEM,
        out_shape=jax.ShapeDtypeStruct((2 * rows, LANES), jnp.float32),
        scratch_shapes=[pltpu.VMEM((MODES * CHUNKS, LANES), jnp.float32)],
        compiler_params=pltpu.CompilerParams(vmem_limit_bytes=16 * 2**20),
        cost_estimate=pl.CostEstimate(
            flops=rows * LANES * 72, bytes_accessed=rows * LANES * 24, transcendentals=0
        ),
    )(seat, arrived, mine, other, weights, decays)


def per_device(tokens, in_weights, short_taps, residues, decays, skip_gain):
    rows = tokens.shape[0]
    part = rows // 2
    blocks = lax.axis_size("ctx")
    ring, lines = RING, LINES
    mine = lax.axis_index("ctx")
    place = mine * lines * ring + lax.axis_index("ch")
    half = lax.axis_index("ch") // ring % 2
    weights = (residues * jnp.sqrt(2.0 * decays / MODES)).T
    rates = decays.T

    def beside(block, step):
        return lax.ppermute(
            block, "ch", [(z * ring + y, (z ^ step) * ring + y) for z in range(lines) for y in range(ring)]
        )

    def onward(block):
        route = []
        for i in range(blocks):
            for z in range(lines):
                for y in range(ring):
                    at = (i * lines + z) * ring
                    route.append((at + y, at + (y + 1 - i % 2 * 2) % ring))
        return lax.ppermute(block, ("ctx", "ch"), route)

    def other_core(block):
        return lax.ppermute(block, "ctx", [(i, i ^ 1) for i in range(blocks)])

    table = np.zeros((2, 2, lines, ring, ring, lines), np.int32)
    for c, z, y, k in np.ndindex(2, lines, ring, lines):
        way = 1 - 2 * c
        places = [y] + [y + way * d for step in range(1, ring // 2) for d in (-step, step)] + [y + ring // 2]
        ids = (z ^ k) * ring + np.array(places) % ring
        count = lines * ring // 2
        table[c, 0, z, y, :, k] = ids
        table[c, 1, z, y, :, k] = ids % count + count * (ids // count != c)
    table = table.transpose(0, 2, 3, 1, 4, 5).reshape(2, lines * ring, -1)[np.arange(blocks) % 2]
    ids = lax.dynamic_index_in_dim(
        jnp.asarray(table.reshape(-1, 2 * lines * ring)), place, 0, keepdims=False
    )

    seat = jnp.stack([mine, half, half]).astype(jnp.int32)
    other_seat = jnp.stack([mine, half, 1 - half]).astype(jnp.int32)

    before = lax.ppermute(tokens[rows - HALO :], "ctx", [(i, i + 1) for i in range(blocks - 1)])
    ordered = tokens.reshape(2, CHUNKS, part // CHUNKS, -1).swapaxes(1, 2).reshape(2, part, -1)
    between = tokens[part - HALO : part]
    low = half == 0
    kept = jnp.concatenate([jnp.where(low, before, between), jnp.where(low, ordered[0], ordered[1])], axis=0)
    given = jnp.concatenate([jnp.where(low, between, before), jnp.where(low, ordered[1], ordered[0])], axis=0)
    nearest = beside(given, 1)
    count = in_weights.shape[1] // 2
    sliced = lax.dynamic_slice_in_dim(in_weights, mine % 2 * count, count, 1)
    values = jnp.concatenate([short_taps.reshape(3 * TAPS, -1), weights, rates, skip_gain[None, :]], axis=0)
    half_weights, values = beside(after(sliced, nearest), 1), beside(values, 1)
    block = jnp.concatenate([kept, nearest, beside(kept, 2), beside(given, 3)], axis=1)

    block = after(after(block, values), sliced)
    straight, turned = onward(block), other_core(block)
    crossed = onward(turned)
    sums, waiting, met = None, [block], 0
    arrived = []
    for step in range(1, ring // 2):
        straight, turned = lax.optimization_barrier((straight, turned))
        crossed, here = lax.optimization_barrier((crossed, straight))
        turned = crossed
        if step == ring // 2 - 1:
            crossed = after(after(crossed, waiting[1]), half_weights)
        straight = onward(straight)
        swapped = other_core(crossed)
        if step < ring // 2 - 1:
            crossed = onward(crossed)
        sums = project(sums, waiting, ids, met, [in_weights])
        arrived += waiting
        met += len(waiting)
        waiting = [here, swapped]
        if step < ring // 2 - 1:
            straight, sums = lax.optimization_barrier((straight, sums))
    half_weights = after(after(half_weights, straight), swapped)
    their_weights = [half_weights, other_core(half_weights)]
    waiting.append(straight)
    pack, sent = local_part(
        None, sums, waiting, seat, ids, met, [in_weights], short_taps, weights, rates, skip_gain[None, :], blocks
    )
    other_pack, sent = local_part(
        sent, None, arrived + waiting, other_seat, ids, ring, their_weights,
        values[: 3 * TAPS].reshape(3, TAPS, -1),
        values[3 * TAPS : 3 * TAPS + MODES],
        values[3 * TAPS + MODES : 3 * TAPS + 2 * MODES],
        values[3 * TAPS + 2 * MODES :],
        blocks,
    )
    other = beside(other_pack, 1)
    groups = [
        [(i * lines + z + q) * ring + y for q in range(2) for i in range(blocks)]
        for z in range(0, lines, 2)
        for y in range(ring)
    ]
    states = lax.all_to_all(
        sent.reshape(2 * blocks, MODES, LANES), ("ctx", "ch"), 0, 0, axis_index_groups=groups, tiled=True
    )
    return final_part(seat, states, pack, other, weights, rates)


def solution(mesh):
    return jax.shard_map(
        per_device,
        mesh=mesh,
        in_specs=(
            P("ctx", "ch"),
            P(None, None, "ch"),
            P(None, None, "ch"),
            P("ch", None),
            P("ch", None),
            P("ch"),
        ),
        out_specs=P("ctx", "ch"),
        check_vma=False,
    )
```
